768 devices in a mesh: lon: 192 (over y_hi, x, z, core), lat: 4 (over y_lo).
Axes of the slice: x: 4, y: 8 (y_hi: 2, y_lo: 4; y = y_hi * 4 + y_lo), z: 12, core: 2. Of those that a mesh axis runs over, the one named last changes fastest.
Arguments:
- gen_prev: float32 [3, 384, 64, 64], P(None, 'lon', 'lat'), may hold values from -3 to 3
- gen_cur: float32 [3, 384, 64, 64], P(None, 'lon', 'lat'), may hold values from -3 to 3
- corr_prev: float32 [3, 384, 64, 64], P(None, 'lon', 'lat'), may hold values from -3 to 3
- corr_cur: float32 [3, 384, 64, 64], P(None, 'lon', 'lat'), may hold values from -3 to 3
- adj_prev: float32 [6, 384, 64, 64], P(None, 'lon', 'lat'), may hold values from -3 to 3
- adj_cur: float32 [6, 384, 64, 64], P(None, 'lon', 'lat'), may hold values from -3 to 3
- courant: float32 [384, 64, 64], P('lon', 'lat'), may hold values from 0.05 to 0.3
- noise: float32 [384, 64, 64], P('lon', 'lat'), may hold values from 0.2 to 2
- station_owner: int32 [256], replicated, may hold values from 0 to 191
- station_cell: int32 [256], replicated, may hold values from 0 to 8191
- pairs: int32 [2, 1024], replicated, may hold values from 0 to 255
- observed: float32 [4, 3, 1024], replicated, may hold values from -3 to 3
- checkpoint: int32 [1], replicated, may hold values from 0 to 255
Outputs:
- corr_last: float32 [3, 384, 64, 64], P(None, 'lon', 'lat')
- adjoint: float32 [6, 384, 64, 64], P(None, 'lon', 'lat')
- kernel: float32 [384, 64, 64], P('lon', 'lat')
The draws below stay inside these ranges and needn't reach their ends.
All inputs are finite; a program needn't handle non-finite values.
Results may differ from the reference program's by a relative error of at most 0.0001.
Values sent between devices are 32-bit elements; how exact they have to be, the bound alone decides.
A program may use at most 32 MiB of HBM per device.

```python
import math
import jax
import jax.numpy as jnp
import numpy as np

CLON = 2
NZ = 64
STEPS = 4
STATIONS = 256
PAIRS = 1024
NLON = 384
NLAT = 64
N_LON = 192


def with_ends(values, stream_key, least, largest):
    shape = values.shape
    spot = [jax.random.randint(jax.random.fold_in(stream_key, axis), (), 0, shape[axis]) for axis in range(len(shape))]
    values = values.at[tuple(spot)].set(least)
    longest = shape.index(max(shape))
    spot[longest] = (spot[longest] + 1) % shape[longest]
    return values.at[tuple(spot)].set(largest)


def block_levels(own_key, dims, cuts, smallest, top_value):
    def one(axis_at, shards_of):
        heights = jax.random.uniform(jax.random.fold_in(jax.random.fold_in(own_key, 6), axis_at), (shards_of,), jnp.float32, smallest / len(cuts), top_value / len(cuts))
        return jnp.repeat(jnp.exp(heights), dims[axis_at] // shards_of).reshape((-1,) + (1,) * (len(dims) - axis_at - 1))

    factor_of = one(*cuts[0])
    for cut in cuts[1:]:
        factor_of = factor_of * one(*cut)
    return factor_of


def rank_bounds(amount, skew):
    loads = [(1 << 20) // math.isqrt(rank ** skew) + 1 for rank in range(1, amount + 1)]
    width = 1 + sum(loads) // (1 << 30)
    return np.cumsum(np.array([max(1, weight // width) for weight in loads]))


def ranked_ids(key, dims, count, skew):
    listing = rank_bounds(count, skew)
    ticket = jax.random.randint(jax.random.fold_in(key, 1), dims, 0, int(listing[count - 1]))
    standing = jnp.searchsorted(jnp.asarray(listing, jnp.int32), ticket, side="right")
    return jax.random.permutation(jax.random.fold_in(key, 2), count)[standing].astype(jnp.int32)


def scatter_about(own_key, dims, scale, bound, pieces=(), dtype=jnp.bfloat16):
    factor_of = block_levels(own_key, dims, pieces, -0.22, 0.18) if pieces else 1.0
    values = jax.random.normal(own_key, dims, jnp.float32) * scale * factor_of
    return jnp.minimum(jnp.maximum(values, -bound), bound).astype(dtype)


def setup_inputs(seed: int = 0) -> dict:
    key_of = jax.random.split(jax.random.key(seed), 14)
    gen_prev = scatter_about(key_of[0], (3, NLON, NLAT, NZ), 0.3, 3.0, ((1, 192), (2, 4)), jnp.float32)
    gen_cur = scatter_about(key_of[1], (3, NLON, NLAT, NZ), 0.3, 3.0, ((1, 192), (2, 4)), jnp.float32)
    corr_prev = scatter_about(key_of[2], (3, NLON, NLAT, NZ), 0.3, 3.0, ((1, 192), (2, 4)), jnp.float32)
    corr_cur = scatter_about(key_of[3], (3, NLON, NLAT, NZ), 0.3, 3.0, ((1, 192), (2, 4)), jnp.float32)
    adj_prev = scatter_about(key_of[4], (6, NLON, NLAT, NZ), 0.3, 3.0, ((1, 192), (2, 4)), jnp.float32)
    adj_cur = scatter_about(key_of[5], (6, NLON, NLAT, NZ), 0.3, 3.0, ((1, 192), (2, 4)), jnp.float32)
    courant = jnp.clip(0.05 + 0.25 * jax.random.uniform(key_of[6], (NLON, NLAT, NZ), jnp.float32) ** block_levels(key_of[6], (NLON, NLAT, NZ), ((0, 192), (1, 4)), -0.2, 0.2), 0.05, 0.3)
    noise = jnp.clip(jnp.exp(math.log(2.0) - 2.3025851 * jax.random.uniform(key_of[7], (NLON, NLAT, NZ), jnp.float32) ** block_levels(key_of[7], (NLON, NLAT, NZ), ((0, 192), (1, 4)), -0.2, 0.2)), 0.2, 2.0)
    station_owner = with_ends(ranked_ids(key_of[8], (STATIONS,), N_LON, 2), jax.random.fold_in(key_of[8], 3), 0, N_LON - 1).astype(jnp.int32)
    station_cell = with_ends(jax.random.randint(key_of[9], (STATIONS,), 0, CLON * NLAT * NZ), jax.random.fold_in(key_of[9], 1), 0, (CLON * NLAT * NZ) - 1).astype(jnp.int32)
    pairs = with_ends(jax.random.randint(key_of[10], (2, PAIRS), 0, STATIONS), jax.random.fold_in(key_of[10], 1), 0, STATIONS - 1).astype(jnp.int32)
    observed = scatter_about(key_of[11], (STEPS, 3, PAIRS), 0.3, 3.0, (), jnp.float32)
    checkpoint = jax.random.randint(key_of[12], (1,), 0, 256).astype(jnp.int32)
    return dict(gen_prev=gen_prev, gen_cur=gen_cur, corr_prev=corr_prev, corr_cur=corr_cur, adj_prev=adj_prev, adj_cur=adj_cur, courant=courant, noise=noise, station_owner=station_owner, station_cell=station_cell, pairs=pairs, observed=observed, checkpoint=checkpoint)


OMEGA = 0.7


def laplace(field):
    along_lon = jnp.roll(field, 1, axis=1) + jnp.roll(field, -1, axis=1)
    padded = jnp.pad(field, ((0, 0), (0, 0), (1, 1), (1, 1)))
    rest = padded[:, :, 2:, 1:-1] + padded[:, :, :-2, 1:-1] + padded[:, :, 1:-1, 2:] + padded[:, :, 1:-1, :-2]
    return along_lon + rest - 6.0 * field


def adjoint_sources(rec_gen, rec_corr, pairs, observed, stations):
    first_station = pairs[0]
    second_station = pairs[1]
    gen_a = jnp.take(rec_gen, first_station, axis=2)
    corr_b = jnp.take(rec_corr, second_station, axis=2)
    misfit = gen_a * corr_b - observed
    src_one = jax.ops.segment_sum(jnp.moveaxis(misfit * corr_b, 2, 0), first_station, num_segments=stations)
    src_two = jax.ops.segment_sum(jnp.moveaxis(misfit * gen_a, 2, 0), second_station, num_segments=stations)
    return src_one, src_two


def reference(gen_prev, gen_cur, corr_prev, corr_cur, adj_prev, adj_cur, courant, noise, station_owner, station_cell, pairs, observed, checkpoint):
    cell_lon = station_owner * CLON + station_cell // (NLAT * NZ)
    cell_lat = (station_cell // NZ) % NLAT
    cell_depth = station_cell % NZ
    phase_start = checkpoint[0].astype(jnp.float32)
    gen_old, gen_now = gen_prev, gen_cur
    corr_old, corr_now = corr_prev, corr_cur
    snapshots = []
    gen_records = []
    corr_records = []
    for n in range(STEPS):
        weight = jnp.cos(OMEGA * (phase_start + n))
        gen_new = 2.0 * gen_now - gen_old + courant * laplace(gen_now)
        corr_new = 2.0 * corr_now - corr_old + courant * laplace(corr_now) + (noise * weight) * gen_now
        gen_old, gen_now = gen_now, gen_new
        corr_old, corr_now = corr_now, corr_new
        snapshots.append(gen_new)
        gen_records.append(gen_new[:, cell_lon, cell_lat, cell_depth])
        corr_records.append(corr_new[:, cell_lon, cell_lat, cell_depth])
    rec_gen = jnp.stack(gen_records)
    rec_corr = jnp.stack(corr_records)
    src_one, src_two = adjoint_sources(rec_gen, rec_corr, pairs, observed, STATIONS)
    adj_old = adj_prev
    adj_now = adj_cur
    kernel = jnp.zeros(courant.shape, jnp.float32)
    for k in range(STEPS):
        later = STEPS - 1 - k
        source = jnp.concatenate([src_one[:, later, :].T, src_two[:, later, :].T], axis=0)
        update = 2.0 * adj_now - adj_old + courant * laplace(adj_now)
        adj_new = update.at[:, cell_lon, cell_lat, cell_depth].add(source)
        kernel = kernel + jnp.sum(adj_new[3:] * snapshots[later], axis=0)
        adj_old, adj_now = adj_now, adj_new
    return corr_now, adj_now, kernel
```

```python
import jax
import jax.numpy as jnp
from jax import lax
from jax.experimental import pallas as pl
from jax.experimental.pallas import tpu as pltpu
from jax.sharding import PartitionSpec as P

OMEGA = 0.7
MESH = pl.DeviceIdType.MESH
F32 = jnp.float32
BF16 = jnp.bfloat16
LONS = 192
LATS = 4
RING_Z = 12
LONG = 2
ROWS = 16
DEEP = 64
TOTAL_LON = LONS * LONG
ROUND = 24
STEPS = 4
STATIONS = 256
PAIRS = 1024
STRIPS = (-1, 0, 1)
OFFSETS = (-2, -1, 0, 1, 2)
GROUPS = ("xc", "y", "z")
PEERS = {"xc": 7, "y": 7, "z": 11}


def place():
    lon = lax.axis_index("lon")
    lat = lax.axis_index("lat")
    return lon, lat, lon // 24, lon % 24


def peer(group, r):
    lon, lat, block, inner = place()
    if group == "xc":
        t = (block % 4 * 2 + inner % 2 + r) % 8
        return ((block // 4 * 4 + t // 2) * 24 + inner // 2 * 2 + t % 2, lat)
    if group == "y":
        t = (block // 4 * 4 + lat + r) % 8
        return ((t // 4 * 4 + block % 4) * 24 + inner, t % 4)
    return (block * 24 + (inner + 2 * r) % 24, lat)


def split2(v):
    high = v.astype(BF16)
    return high, (v - high.astype(F32)).astype(BF16)


def split3(v):
    high = v.astype(BF16)
    rest = v - high.astype(F32)
    mid = rest.astype(BF16)
    return high, mid, (rest - mid.astype(F32)).astype(BF16)


def dot(a, b):
    return lax.dot_general(a, b, (((1,), (0,)), ((), ())), preferred_element_type=F32)


def dot_t(a, b):
    return lax.dot_general(a, b, (((1,), (1,)), ((), ())), preferred_element_type=F32)


def laplace(cur, p, lane):
    x = cur.get(p)
    low = cur.get(p - 1)
    high = cur.get(p + 1)
    zero = jnp.zeros((ROUND, 128), F32)
    sides = jnp.where(
        lane >= DEEP, zero if low is None else low, zero if high is None else high
    )
    if x is None:
        return pltpu.roll(sides, DEEP, 1)
    along_lon = pltpu.roll(x + sides, DEEP, 1)
    deeper = jnp.where(lane % DEEP == 0, 0.0, pltpu.roll(x, 1, 1))
    higher = jnp.where(lane % DEEP == DEEP - 1, 0.0, pltpu.roll(x, 127, 1))
    north = pltpu.roll(x, 1, 0)
    south = pltpu.roll(x, ROUND - 1, 0)
    return along_lon + (north + south + deeper + higher) - 6.0 * x


def advance(cur, old, speed, pairs, lane):
    new = {}
    for p in pairs:
        v = speed[p] * laplace(cur, p, lane)
        if p in cur:
            v = v + 2.0 * cur[p]
        if p in old:
            v = v - old[p]
        new[p] = v
    return new


def body(
    gen_prev,
    gen_cur,
    corr_prev,
    corr_cur,
    adj_prev,
    adj_cur,
    courant,
    noise,
    owner,
    cell,
    pairs,
    observed,
    checkpoint,
    out_corr,
    out_adj,
    out_kernel,
    st_fields,
    st_cn,
    v_owner,
    v_cell,
    v_pairs,
    v_obs,
    e0,
    e1,
    e2,
    e3,
    e4,
    c0,
    c1,
    c2,
    c3,
    c4,
    cn_strip,
    strip_out,
    strip_in,
    row_out,
    row_in,
    snap,
    adj_one,
    depth_hot,
    first_hot,
    second_hot,
    obs,
    chunks,
    total,
    slots,
    gathered,
    rec,
    load_sem,
    cn_sem,
    bulk_sem,
    group_sem,
):
    lon, lat, block, inner = place()
    ext = {-2: e0, -1: e1, 0: e2, 1: e3, 2: e4}
    cn = {-2: c0, -1: c1, 0: c2, 1: c3, 2: c4}
    loads = []
    sources = [
        (courant, st_cn.at[0]),
        (noise, st_cn.at[1]),
        (gen_cur, st_fields.at[0, pl.ds(0, 3)]),
        (corr_cur, st_fields.at[0, pl.ds(3, 3)]),
        (gen_prev, st_fields.at[1, pl.ds(0, 3)]),
        (corr_prev, st_fields.at[1, pl.ds(3, 3)]),
        (adj_cur, st_fields.at[0, pl.ds(6, 6)]),
        (adj_prev, st_fields.at[1, pl.ds(6, 6)]),
        (owner, v_owner),
        (cell, v_cell),
        (pairs, v_pairs),
        (observed, v_obs),
    ]
    for i, (src, dst) in enumerate(sources):
        copy = pltpu.make_async_copy(src, dst, load_sem.at[i])
        copy.start()
        loads.append(copy)
    barrier = pltpu.get_barrier_semaphore()
    greeted = 0
    for dl in OFFSETS:
        for da in STRIPS:
            if dl or da:
                pl.semaphore_signal(
                    barrier,
                    inc=1,
                    device_id=((lon + dl + LONS) % LONS, (lat + da + LATS) % LATS),
                    device_id_type=MESH,
                )
                greeted += 1
    for group in GROUPS:

        def greet(r, carry, group=group):
            pl.semaphore_signal(barrier, inc=1, device_id=peer(group, r), device_id_type=MESH)
            return carry

        lax.fori_loop(1, PEERS[group] + 1, greet, 0)
        greeted += PEERS[group]

    lane = lax.broadcasted_iota(jnp.int32, (ROUND, 128), 1)
    sub8 = lax.broadcasted_iota(jnp.int32, (8, 128), 0)
    zeros8 = jnp.zeros((8, 128), F32)

    loads[0].wait()
    loads[1].wait()
    for ch in range(2):
        c2[ch, 0:ROWS] = jnp.concatenate([st_cn[ch, 0], st_cn[ch, 1]], axis=1)
    for k in range(2, 8):
        loads[k].wait()

    def pack(ch, carry):
        for t in range(2):
            wide = jnp.concatenate([st_fields[t, ch, 0], st_fields[t, ch, 1]], axis=1)
            e2[t, ch, 0:ROWS] = wide
        now = e2[0, ch, 0:ROWS]
        old = e2[1, ch, 0:ROWS]
        strip_out[0, ch] = jnp.where(sub8 < 4, now[0:8], pltpu.roll(old[0:8], 4, 0))
        strip_out[1, ch] = jnp.where(sub8 < 4, pltpu.roll(now[8:16], 4, 0), old[8:16])
        row_out[0, pl.ds(ch, 1)] = now[0:1]
        row_out[1, pl.ds(ch, 1)] = now[ROWS - 1 : ROWS]
        return carry

    lax.fori_loop(0, 12, pack, 0)
    for k in range(8, 12):
        loads[k].wait()

    pl.semaphore_wait(barrier, greeted)

    has_low = lat > 0
    has_high = lat < LATS - 1

    def target(dl, da):
        return ((lon + dl + LONS) % LONS, (lat + da + LATS) % LATS)

    def remote(src, dst, sems, k, dl, da):
        return pltpu.make_async_remote_copy(
            src, dst, sems.at[0, k], sems.at[1, k], device_id=target(dl, da), device_id_type=MESH
        )

    cn_copies = []
    for dl in (-1, 1, -2, 2):
        cn_copies.append(
            (
                remote(
                    c2.at[:, pl.ds(0, ROWS)],
                    cn[-dl].at[:, pl.ds(0, ROWS)],
                    cn_sem,
                    len(cn_copies),
                    dl,
                    0,
                ),
                0,
            )
        )
    for dl in (0, -1, 1, -2, 2):
        for da in (-1, 1):
            cn_copies.append(
                (
                    remote(
                        c2.at[:, pl.ds(0 if da < 0 else 8, 8)],
                        cn_strip.at[0 if da < 0 else 1, 2 - dl],
                        cn_sem,
                        len(cn_copies),
                        dl,
                        da,
                    ),
                    da,
                )
            )
    bulk = []
    for dl in (-1, 1, -2, 2):
        bulk.append(
            (
                remote(
                    e2.at[:, :, pl.ds(0, ROWS)],
                    ext[-dl].at[:, :, pl.ds(0, ROWS)],
                    bulk_sem,
                    len(bulk),
                    dl,
                    0,
                ),
                0,
            )
        )
    for dl in (0, -1, 1):
        for da in (-1, 1):
            d = 0 if da < 0 else 1
            bulk.append(
                (
                    remote(strip_out.at[d], strip_in.at[d, 1 - dl], bulk_sem, len(bulk), dl, da),
                    da,
                )
            )
    for dl in (-2, 2):
        for da in (-1, 1):
            d = 0 if da < 0 else 1
            bulk.append(
                (
                    remote(
                        row_out.at[d],
                        row_in.at[d, 0 if dl > 0 else 1],
                        bulk_sem,
                        len(bulk),
                        dl,
                        da,
                    ),
                    da,
                )
            )

    def sends(da):
        return has_low if da < 0 else has_high

    def receives(da):
        return has_high if da < 0 else has_low

    for copies in (cn_copies, bulk):
        for copy, da in copies:
            if da:
                pl.when(sends(da))(copy.start)
            else:
                copy.start()

    def take(copies):
        for copy, da in copies:
            if da:
                pl.when(receives(da))(copy.wait_recv)
            else:
                copy.wait_recv()

    own = v_owner[...]
    where_in = v_cell[...]
    slon = own * LONG + where_in // (LATS * ROWS * DEEP)
    slat = where_in // DEEP % (LATS * ROWS)
    slane = where_in // (LATS * ROWS * DEEP) * DEEP + where_in % DEEP
    rel_lon = (slon - lon * LONG + 4 + TOTAL_LON) % TOTAL_LON
    rel_lat = slat - lat * ROWS
    near = (rel_lon < 10) & (rel_lat >= -4) & (rel_lat < ROWS + 4)
    row24 = jnp.where(rel_lat < 0, rel_lat + ROUND, rel_lat)
    spot = jnp.where(near, rel_lon // 2 * ROUND + row24, -1)
    spot = jnp.broadcast_to(spot, (ROUND, STATIONS))
    row_id = lax.broadcasted_iota(jnp.int32, (ROUND, STATIONS), 0)
    lanes = lax.broadcasted_iota(jnp.int32, (128, STATIONS), 0)
    hot = jnp.where(lanes == slane, 1.0, 0.0).astype(BF16)
    depth_hot[0:128] = hot
    depth_hot[128:256] = hot

    phase = checkpoint[0].astype(F32)
    weights = [jnp.cos(jnp.full((ROUND, 128), OMEGA * (phase + n), F32)) for n in range(STEPS)]

    take(cn_copies)
    for p in OFFSETS:
        for ch in range(2):
            above = jnp.where(has_high, cn_strip[0, p + 2, ch], zeros8)
            below = jnp.where(has_low, cn_strip[1, p + 2, ch], zeros8)
            cn[p][ch, ROWS:ROUND] = jnp.where(sub8 < 4, above, below)
    reach = ((-1, 0, 1), (-1, 0, 1), OFFSETS, OFFSETS)

    def responses(i, carry):
        pad = jnp.zeros((8, 128), F32)

        def own_cells(t, ch):
            return jnp.concatenate([e2[t, ch, 0:ROWS], pad], axis=0)

        speed = {p: cn[p][0] for p in OFFSETS}
        gen = {0: own_cells(0, i)}
        gen_old = {0: own_cells(1, i)}
        corr = {0: own_cells(0, 3 + i)}
        corr_old = {0: own_cells(1, 3 + i)}
        for n in range(STEPS):
            gen_new = advance(gen, gen_old, speed, reach[n], lane)
            corr_new = advance(corr, corr_old, speed, reach[n], lane)
            for p in reach[n]:
                if p in gen:
                    corr_new[p] = corr_new[p] + (cn[p][1] * weights[n]) * gen[p]
            gen_old, gen = gen, gen_new
            corr_old, corr = corr, corr_new
            tiles = [field[p] for field in (gen, corr) for p in reach[n]]
            stack = jnp.concatenate(tiles, axis=0)
            picked = dot(jnp.concatenate(split2(stack), axis=1), depth_hot[...])
            for f in range(2):
                summed = jnp.zeros((ROUND, STATIONS), F32)
                for k, p in enumerate(reach[n]):
                    at = (f * len(reach[n]) + k) * ROUND
                    summed = summed + jnp.where(
                        spot == row_id + (p + 2) * ROUND, picked[at : at + ROUND], 0.0
                    )
                line = jnp.sum(summed, axis=0, keepdims=True)
                chunks[2 * n + f, pl.ds(i, 1)] = line[:, 0:128]
                chunks[2 * n + f, pl.ds(3 + i, 1)] = line[:, 128:256]
        return carry

    for j in range(8):
        chunks[j, 6:8] = jnp.zeros((2, 128), F32)
    lax.fori_loop(0, 3, responses, 0)

    me_xc = block % 4 * 2 + inner % 2

    def post(k, group, src_of, dst_of):
        def one(r, carry):
            pltpu.make_async_remote_copy(
                src_of(r),
                dst_of(r),
                group_sem.at[0, k],
                group_sem.at[1, k],
                device_id=peer(group, r),
                device_id_type=MESH,
            ).start()
            return carry

        lax.fori_loop(1, PEERS[group] + 1, one, 0)

    def drain(k, group, side):
        ref = slots.at[k % 3, pl.ds(0, PEERS[group])]
        pltpu.make_async_copy(ref, ref, group_sem.at[side, k]).wait()

    post(0, "xc", lambda r: chunks.at[(me_xc + r) % 8], lambda r: slots.at[0, r - 1])

    take(bulk)

    def assemble(ch, carry):
        for p in STRIPS:
            above = jnp.where(has_high, strip_in[0, p + 1, ch], zeros8)
            below = jnp.where(has_low, strip_in[1, p + 1, ch], zeros8)
            ext[p][0, ch, ROWS:ROUND] = jnp.where(sub8 < 4, above, pltpu.roll(below, 4, 0))
            ext[p][1, ch, ROWS:ROUND] = jnp.where(sub8 < 4, pltpu.roll(above, 4, 0), below)
        for k, p in enumerate((-2, 2)):
            above = jnp.where(has_high, row_in[0, k, pl.ds(ch, 1)], 0.0)
            below = jnp.where(has_low, row_in[1, k, pl.ds(ch, 1)], 0.0)
            ext[p][0, ch, ROWS:ROUND] = jnp.where(
                sub8 == 0, above, jnp.where(sub8 == 7, below, 0.0)
            )
            ext[p][1, ch, ROWS:ROUND] = zeros8
        return carry

    lax.fori_loop(0, 12, assemble, 0)

    shrink = (OFFSETS, (-1, 0, 1), (-1, 0, 1), (0,))

    def wavefields(i, carry):
        speed = {p: cn[p][0] for p in OFFSETS}
        gen = {p: ext[p][0, i] for p in OFFSETS}
        gen_old = {p: ext[p][1, i] for p in OFFSETS}
        corr = {p: ext[p][0, 3 + i] for p in OFFSETS}
        corr_old = {p: ext[p][1, 3 + i] for p in OFFSETS}
        for n in range(STEPS):
            gen_new = advance(gen, gen_old, speed, shrink[n], lane)
            corr_new = advance(corr, corr_old, speed, shrink[n], lane)
            for p in shrink[n]:
                corr_new[p] = corr_new[p] + (cn[p][1] * weights[n]) * gen[p]
            gen_old, gen = gen, gen_new
            corr_old, corr = corr, corr_new
            snap[n, i] = gen[0][0:ROWS]
        last = corr[0][0:ROWS]
        out_corr[i, 0] = last[:, 0:DEEP]
        out_corr[i, 1] = last[:, DEEP:128]
        return carry

    lax.fori_loop(0, 3, wavefields, 0)

    def gather_sum(k, group, own_part):
        drain(k, group, 1)
        part = own_part
        for r in range(PEERS[group]):
            part = part + slots[k, r]
        total[k] = part
        return part

    gather_sum(0, "xc", chunks[me_xc])
    post(1, "y", lambda r: total.at[0], lambda r: slots.at[1, r - 1])

    def first_adjoint(ch, carry):
        speed = {p: cn[p][0] for p in OFFSETS}
        now = {p: ext[p][0, ch] for p in OFFSETS}
        old = {p: ext[p][1, ch] for p in OFFSETS}
        new = advance(now, old, speed, OFFSETS, lane)
        for p in OFFSETS:
            adj_one[ch, p + 2] = new[p]
        return carry

    lax.fori_loop(0, 6, lambda c, carry: first_adjoint(c + 6, carry), 0)
    gather_sum(1, "y", total[0])
    post(2, "z", lambda r: total.at[1], lambda r: slots.at[2, r - 1])
    ids = lax.broadcasted_iota(jnp.int32, (STATIONS, PAIRS), 0)
    first_hot[...] = jnp.where(ids == v_pairs[0:1], 1.0, 0.0).astype(BF16)
    second_hot[...] = jnp.where(ids == v_pairs[1:2], 1.0, 0.0).astype(BF16)
    rec[...] = jnp.zeros(rec.shape, F32)
    obs[...] = jnp.zeros(obs.shape, F32)
    for n in range(STEPS):
        obs[3 * n : 3 * n + 3] = v_obs[n]
    gathered[me_xc] = gather_sum(2, "z", total[1])
    post(3, "xc", lambda r: total.at[2], lambda r: gathered.at[me_xc])
    ref = gathered.at[pl.ds(0, 7)]
    pltpu.make_async_copy(ref, ref, group_sem.at[1, 3]).wait()

    for n in range(STEPS):
        for f in range(2):
            tile = gathered[2 * n + f]
            rec[f, 3 * n : 3 * n + 3, 0:128] = tile[0:3]
            rec[f, 3 * n : 3 * n + 3, 128:256] = tile[3:6]

    def thirds(v, hot, times):
        stack = jnp.concatenate(split3(v), axis=0)
        got = times(stack, hot)
        return got[0:16] + got[16:32] + got[32:48]

    first = first_hot[...]
    second = second_hot[...]
    gen_a = thirds(rec[0], first, dot)
    corr_b = thirds(rec[1], second, dot)
    misfit = gen_a * corr_b - obs[...]
    src = (thirds(misfit * corr_b, first, dot_t), thirds(misfit * gen_a, second, dot_t))

    speed = {p: cn[p][0] for p in OFFSETS}
    hot = depth_hot[0:128]
    now = {}
    old = {}
    for c in range(6):
        now[c] = {p: adj_one[6 + c, p + 2] for p in OFFSETS}
        old[c] = {p: ext[p][0, 6 + c] for p in OFFSETS}
    kernel = jnp.zeros((ROWS, 128), F32)
    halves = [split2(s) for s in src]
    for k in range(STEPS):
        later = STEPS - 1 - k
        for c in range(6):
            if k:
                new = advance(now[c], old[c], speed, shrink[k], lane)
                old[c], now[c] = now[c], new
            line = 3 * later + c % 3
            lhs = []
            for h in halves[c // 3]:
                mine = jnp.broadcast_to(h[line : line + 1].astype(F32), (ROUND, STATIONS))
                for p in shrink[k]:
                    lhs.append(
                        jnp.where(spot == row_id + (p + 2) * ROUND, mine, 0.0).astype(BF16)
                    )
            put = dot_t(jnp.concatenate(lhs, axis=0), hot)
            count = len(shrink[k])
            for j, p in enumerate(shrink[k]):
                now[c][p] = (
                    now[c][p]
                    + put[j * ROUND : (j + 1) * ROUND]
                    + put[(count + j) * ROUND : (count + j + 1) * ROUND]
                )
            if c >= 3:
                kernel = kernel + now[c][0][0:ROWS] * snap[later, c - 3]
    for c in range(6):
        last = now[c][0][0:ROWS]
        out_adj[c, 0] = last[:, 0:DEEP]
        out_adj[c, 1] = last[:, DEEP:128]
    out_kernel[0] = kernel[:, 0:DEEP]
    out_kernel[1] = kernel[:, DEEP:128]

    for copies in (cn_copies, bulk):
        for copy, da in copies:
            if da:
                pl.when(sends(da))(copy.wait_send)
            else:
                copy.wait_send()
    for k, group in enumerate(("xc", "y", "z", "xc")):
        drain(k, group, 0)


def shards(
    gen_prev,
    gen_cur,
    corr_prev,
    corr_cur,
    adj_prev,
    adj_cur,
    courant,
    noise,
    station_owner,
    station_cell,
    pairs,
    observed,
    checkpoint,
):
    anywhere = pl.BlockSpec(memory_space=pl.ANY)
    vmem = pl.BlockSpec(memory_space=pltpu.VMEM)
    ext = pltpu.VMEM((2, 12, ROUND, 128), F32)
    cn = pltpu.VMEM((2, ROUND, 128), F32)
    return pl.pallas_call(
        body,
        name="window",
        out_shape=(
            jax.ShapeDtypeStruct((3, LONG, ROWS, DEEP), F32),
            jax.ShapeDtypeStruct((6, LONG, ROWS, DEEP), F32),
            jax.ShapeDtypeStruct((LONG, ROWS, DEEP), F32),
        ),
        in_specs=[anywhere] * 12 + [pl.BlockSpec(memory_space=pltpu.SMEM)],
        out_specs=(vmem, vmem, vmem),
        scratch_shapes=[
            pltpu.VMEM((2, 12, LONG, ROWS, DEEP), F32),
            pltpu.VMEM((2, LONG, ROWS, DEEP), F32),
            pltpu.VMEM((1, STATIONS), jnp.int32),
            pltpu.VMEM((1, STATIONS), jnp.int32),
            pltpu.VMEM((2, PAIRS), jnp.int32),
            pltpu.VMEM((STEPS, 3, PAIRS), F32),
            ext,
            ext,
            ext,
            ext,
            ext,
            cn,
            cn,
            cn,
            cn,
            cn,
            pltpu.VMEM((2, 5, 2, 8, 128), F32),
            pltpu.VMEM((2, 12, 8, 128), F32),
            pltpu.VMEM((2, 3, 12, 8, 128), F32),
            pltpu.VMEM((2, 16, 128), F32),
            pltpu.VMEM((2, 2, 16, 128), F32),
            pltpu.VMEM((STEPS, 3, ROWS, 128), F32),
            pltpu.VMEM((12, 5, ROUND, 128), F32),
            pltpu.VMEM((256, STATIONS), BF16),
            pltpu.VMEM((STATIONS, PAIRS), BF16),
            pltpu.VMEM((STATIONS, PAIRS), BF16),
            pltpu.VMEM((16, PAIRS), F32),
            pltpu.VMEM((8, 8, 128), F32),
            pltpu.VMEM((3, 8, 128), F32),
            pltpu.VMEM((3, 11, 8, 128), F32),
            pltpu.VMEM((8, 8, 128), F32),
            pltpu.VMEM((2, 16, STATIONS), F32),
            pltpu.SemaphoreType.DMA((12,)),
            pltpu.SemaphoreType.DMA((2, 14)),
            pltpu.SemaphoreType.DMA((2, 14)),
            pltpu.SemaphoreType.DMA((2, 4)),
        ],
        compiler_params=pltpu.CompilerParams(
            collective_id=0, has_side_effects=True, vmem_limit_bytes=48 * 1024 * 1024
        ),
    )(
        gen_prev,
        gen_cur,
        corr_prev,
        corr_cur,
        adj_prev,
        adj_cur,
        courant,
        noise,
        station_owner.reshape(1, STATIONS),
        station_cell.reshape(1, STATIONS),
        pairs,
        observed,
        checkpoint,
    )


def solution(mesh):
    field = P(None, "lon", "lat", None)
    cells = P("lon", "lat", None)
    return jax.shard_map(
        shards,
        mesh=mesh,
        in_specs=(field,) * 6 + (cells,) * 2 + (P(),) * 5,
        out_specs=(field, field, cells),
        check_vma=False,
    )
```

```python
import jax
import jax.numpy as jnp
from jax import lax
from jax.experimental import pallas as pl
from jax.experimental.pallas import tpu as pltpu
from jax.sharding import PartitionSpec as P

OMEGA = 0.7
MESH = pl.DeviceIdType.MESH
F32 = jnp.float32
BF16 = jnp.bfloat16
LONS = 192
LATS = 4
RING_Z = 12
LONG = 2
ROWS = 16
DEEP = 64
TOTAL_LON = LONS * LONG
ROUND = 24
STEPS = 4
STATIONS = 256
PAIRS = 1024
STRIPS = (-1, 0, 1)
OFFSETS = (-2, -1, 0, 1, 2)
GROUPS = ("xc", "y", "z")
PEERS = {"xc": 7, "y": 7, "z": 11}


def place():
    lon = lax.axis_index("lon")
    lat = lax.axis_index("lat")
    return lon, lat, lon // 24, lon % 24


def peer(group, r):
    lon, lat, block, inner = place()
    if group == "xc":
        t = (block % 4 * 2 + inner % 2 + r) % 8
        return ((block // 4 * 4 + t // 2) * 24 + inner // 2 * 2 + t % 2, lat)
    if group == "y":
        t = (block // 4 * 4 + lat + r) % 8
        return ((t // 4 * 4 + block % 4) * 24 + inner, t % 4)
    return (block * 24 + (inner + 2 * r) % 24, lat)


def split2(v):
    high = v.astype(BF16)
    return high, (v - high.astype(F32)).astype(BF16)


def split3(v):
    high = v.astype(BF16)
    rest = v - high.astype(F32)
    mid = rest.astype(BF16)
    return high, mid, (rest - mid.astype(F32)).astype(BF16)


def dot(a, b):
    return lax.dot_general(a, b, (((1,), (0,)), ((), ())), preferred_element_type=F32)


def dot_t(a, b):
    return lax.dot_general(a, b, (((1,), (1,)), ((), ())), preferred_element_type=F32)


def laplace(cur, p, lane):
    x = cur.get(p)
    low = cur.get(p - 1)
    high = cur.get(p + 1)
    zero = jnp.zeros((ROUND, 128), F32)
    sides = jnp.where(
        lane >= DEEP, zero if low is None else low, zero if high is None else high
    )
    if x is None:
        return pltpu.roll(sides, DEEP, 1)
    along_lon = pltpu.roll(x + sides, DEEP, 1)
    deeper = jnp.where(lane % DEEP == 0, 0.0, pltpu.roll(x, 1, 1))
    higher = jnp.where(lane % DEEP == DEEP - 1, 0.0, pltpu.roll(x, 127, 1))
    north = pltpu.roll(x, 1, 0)
    south = pltpu.roll(x, ROUND - 1, 0)
    return along_lon + (north + south + deeper + higher) - 6.0 * x


def advance(cur, old, speed, pairs, lane):
    new = {}
    for p in pairs:
        v = speed[p] * laplace(cur, p, lane)
        if p in cur:
            v = v + 2.0 * cur[p]
        if p in old:
            v = v - old[p]
        new[p] = v
    return new


def body(
    gen_prev,
    gen_cur,
    corr_prev,
    corr_cur,
    adj_prev,
    adj_cur,
    courant,
    noise,
    owner,
    cell,
    pairs,
    observed,
    checkpoint,
    out_corr,
    out_adj,
    out_kernel,
    st_fields,
    st_cn,
    v_owner,
    v_cell,
    v_pairs,
    v_obs,
    fields,
    c0,
    c1,
    c2,
    c3,
    c4,
    cn_strip,
    side_out,
    side_in,
    row_out,
    row_in,
    depth_hot,
    first_hot,
    second_hot,
    obs,
    chunks,
    total,
    slots,
    gathered,
    rec,
    load_sem,
    cn_sem,
    halo_sem,
    group_sem,
):
    lon, lat, block, inner = place()
    cn = {-2: c0, -1: c1, 0: c2, 1: c3, 2: c4}
    loads = []
    sources = [
        (courant, st_cn.at[0]),
        (noise, st_cn.at[1]),
        (gen_cur, st_fields.at[0, pl.ds(0, 3)]),
        (corr_cur, st_fields.at[0, pl.ds(3, 3)]),
        (gen_prev, st_fields.at[1, pl.ds(0, 3)]),
        (corr_prev, st_fields.at[1, pl.ds(3, 3)]),
        (adj_cur, st_fields.at[0, pl.ds(6, 6)]),
        (adj_prev, st_fields.at[1, pl.ds(6, 6)]),
        (owner, v_owner),
        (cell, v_cell),
        (pairs, v_pairs),
        (observed, v_obs),
    ]
    for i, (src, dst) in enumerate(sources):
        copy = pltpu.make_async_copy(src, dst, load_sem.at[i])
        copy.start()
        loads.append(copy)
    barrier = pltpu.get_barrier_semaphore()
    greeted = 0
    for dl in OFFSETS:
        for da in STRIPS:
            if dl or da:
                pl.semaphore_signal(
                    barrier,
                    inc=1,
                    device_id=((lon + dl + LONS) % LONS, (lat + da + LATS) % LATS),
                    device_id_type=MESH,
                )
                greeted += 1
    for group in GROUPS:

        def greet(r, carry, group=group):
            pl.semaphore_signal(barrier, inc=1, device_id=peer(group, r), device_id_type=MESH)
            return carry

        lax.fori_loop(1, PEERS[group] + 1, greet, 0)
        greeted += PEERS[group]

    lane = lax.broadcasted_iota(jnp.int32, (ROUND, 128), 1)
    sub8 = lax.broadcasted_iota(jnp.int32, (8, 128), 0)
    zeros8 = jnp.zeros((8, 128), F32)

    loads[0].wait()
    loads[1].wait()
    for ch in range(2):
        c2[ch, 0:ROWS] = jnp.concatenate([st_cn[ch, 0], st_cn[ch, 1]], axis=1)
    pl.semaphore_wait(barrier, greeted)

    has_low = lat > 0
    has_high = lat < LATS - 1

    def target(dl, da):
        return ((lon + dl + LONS) % LONS, (lat + da + LATS) % LATS)

    def remote(src, dst, sems, k, dl, da):
        return pltpu.make_async_remote_copy(
            src, dst, sems.at[0, k], sems.at[1, k], device_id=target(dl, da), device_id_type=MESH
        )

    cn_copies = []
    for dl in (-1, 1, -2, 2):
        cn_copies.append(
            (
                remote(
                    c2.at[:, pl.ds(0, ROWS)],
                    cn[-dl].at[:, pl.ds(0, ROWS)],
                    cn_sem,
                    len(cn_copies),
                    dl,
                    0,
                ),
                0,
            )
        )
    for dl in (0, -1, 1, -2, 2):
        for da in (-1, 1):
            cn_copies.append(
                (
                    remote(
                        c2.at[:, pl.ds(0 if da < 0 else 8, 8)],
                        cn_strip.at[0 if da < 0 else 1, 2 - dl],
                        cn_sem,
                        len(cn_copies),
                        dl,
                        da,
                    ),
                    da,
                )
            )

    def sends(da):
        return has_low if da < 0 else has_high

    def receives(da):
        return has_high if da < 0 else has_low

    def go(copies):
        for copy, da in copies:
            if da:
                pl.when(sends(da))(copy.start)
            else:
                copy.start()

    def take(copies):
        for copy, da in copies:
            if da:
                pl.when(receives(da))(copy.wait_recv)
            else:
                copy.wait_recv()

    go(cn_copies)

    for k in range(2, 8):
        loads[k].wait()

    def pack(ch, carry):
        for t in range(2):
            wide = jnp.concatenate([st_fields[t, ch, 0], st_fields[t, ch, 1]], axis=1)
            fields[1 - t, ch] = wide
        return carry

    lax.fori_loop(0, 12, pack, 0)
    lane16 = lane[0:ROWS]
    row16 = lax.broadcasted_iota(jnp.int32, (ROWS, 128), 0)

    def halo(n):
        copies = []
        for d, dl in enumerate((-1, 1)):
            copies.append(
                (remote(side_out.at[n, d], side_in.at[n, d], halo_sem.at[n], len(copies), dl, 0), 0)
            )
        for d, da in enumerate((-1, 1)):
            copies.append(
                (remote(row_out.at[n, d], row_in.at[n, d], halo_sem.at[n], len(copies), 0, da), da)
            )
        return copies

    def send_halo(n):
        def fill(c, carry):
            one = fields[n + 1, c]
            two = fields[n + 1, c + 6]
            turned = pltpu.roll(two, DEEP, 1)
            side_out[n, 0, c] = jnp.where(lane16 < DEEP, one, turned)
            side_out[n, 1, c] = jnp.where(lane16 < DEEP, turned, one)
            for half, x in ((0, one), (6, two)):
                row_out[n, 0, pl.ds(c + half, 1)] = x[0:1]
                row_out[n, 1, pl.ds(c + half, 1)] = x[ROWS - 1 : ROWS]
            return carry

        lax.fori_loop(0, 6, fill, 0)
        copies = halo(n)
        go(copies)
        return copies

    halos = [send_halo(0)]
    for k in range(8, 12):
        loads[k].wait()

    own = v_owner[...]
    where_in = v_cell[...]
    slon = own * LONG + where_in // (LATS * ROWS * DEEP)
    slat = where_in // DEEP % (LATS * ROWS)
    slane = where_in // (LATS * ROWS * DEEP) * DEEP + where_in % DEEP
    rel_lon = (slon - lon * LONG + 4 + TOTAL_LON) % TOTAL_LON
    rel_lat = slat - lat * ROWS
    near = (rel_lon < 10) & (rel_lat >= -4) & (rel_lat < ROWS + 4)
    row24 = jnp.where(rel_lat < 0, rel_lat + ROUND, rel_lat)
    spot = jnp.where(near, rel_lon // 2 * ROUND + row24, -1)
    spot = jnp.broadcast_to(spot, (ROUND, STATIONS))
    row_id = lax.broadcasted_iota(jnp.int32, (ROUND, STATIONS), 0)
    lanes = lax.broadcasted_iota(jnp.int32, (128, STATIONS), 0)
    hot = jnp.where(lanes == slane, 1.0, 0.0).astype(BF16)
    depth_hot[0:128] = hot
    depth_hot[128:256] = hot

    phase = checkpoint[0].astype(F32)
    weights = [jnp.cos(jnp.full((ROUND, 128), OMEGA * (phase + n), F32)) for n in range(STEPS)]

    ids = lax.broadcasted_iota(jnp.int32, (STATIONS, PAIRS), 0)
    first_hot[...] = jnp.where(ids == v_pairs[0:1], 1.0, 0.0).astype(BF16)
    second_hot[...] = jnp.where(ids == v_pairs[1:2], 1.0, 0.0).astype(BF16)
    rec[...] = jnp.zeros(rec.shape, F32)
    obs[...] = jnp.zeros(obs.shape, F32)
    for n in range(STEPS):
        for i in range(3):
            obs[3 * n + i : 3 * n + i + 1] = v_obs[i, n : n + 1]
    for j in range(8):
        chunks[j, 6:8] = jnp.zeros((2, 128), F32)

    take(cn_copies)
    for p in OFFSETS:
        for ch in range(2):
            above = jnp.where(has_high, cn_strip[0, p + 2, ch], zeros8)
            below = jnp.where(has_low, cn_strip[1, p + 2, ch], zeros8)
            cn[p][ch, ROWS:ROUND] = jnp.where(sub8 < 4, above, below)
    reach = ((-1, 0, 1), (-1, 0, 1), OFFSETS, OFFSETS)

    def responses(i, carry):
        pad = jnp.zeros((8, 128), F32)

        def own_cells(t, ch):
            return jnp.concatenate([fields[1 - t, ch], pad], axis=0)

        speed = {p: cn[p][0] for p in OFFSETS}
        gen = {0: own_cells(0, i)}
        gen_old = {0: own_cells(1, i)}
        corr = {0: own_cells(0, 3 + i)}
        corr_old = {0: own_cells(1, 3 + i)}
        for n in range(STEPS):
            gen_new = advance(gen, gen_old, speed, reach[n], lane)
            corr_new = advance(corr, corr_old, speed, reach[n], lane)
            for p in reach[n]:
                if p in gen:
                    corr_new[p] = corr_new[p] + (cn[p][1] * weights[n]) * gen[p]
            gen_old, gen = gen, gen_new
            corr_old, corr = corr, corr_new
            tiles = [field[p] for field in (gen, corr) for p in reach[n]]
            stack = jnp.concatenate(tiles, axis=0)
            picked = dot(jnp.concatenate(split2(stack), axis=1), depth_hot[...])
            for f in range(2):
                summed = jnp.zeros((ROUND, STATIONS), F32)
                for k, p in enumerate(reach[n]):
                    at = (f * len(reach[n]) + k) * ROUND
                    summed = summed + jnp.where(
                        spot == row_id + (p + 2) * ROUND, picked[at : at + ROUND], 0.0
                    )
                line = jnp.sum(summed, axis=0, keepdims=True)
                chunks[2 * n + f, pl.ds(i, 1)] = line[:, 0:128]
                chunks[2 * n + f, pl.ds(3 + i, 1)] = line[:, 128:256]
        return carry

    lax.fori_loop(0, 3, responses, 0)

    me_xc = block % 4 * 2 + inner % 2

    def post(k, group, src_of, dst_of):
        def one(r, carry):
            pltpu.make_async_remote_copy(
                src_of(r),
                dst_of(r),
                group_sem.at[0, k],
                group_sem.at[1, k],
                device_id=peer(group, r),
                device_id_type=MESH,
            ).start()
            return carry

        lax.fori_loop(1, PEERS[group] + 1, one, 0)

    def drain(k, group, side):
        ref = slots.at[k % 3, pl.ds(0, PEERS[group])]
        pltpu.make_async_copy(ref, ref, group_sem.at[side, k]).wait()

    post(0, "xc", lambda r: chunks.at[(me_xc + r) % 8], lambda r: slots.at[0, r - 1])

    def step(n):
        take(halos[n])
        speed = c2[0, 0:ROWS]

        def one(c, twice):
            x = fields[n + 1, c]
            low = side_in[n, 1, c - 6 if twice else c]
            high = side_in[n, 0, c - 6 if twice else c]
            if twice:
                along_lon = pltpu.roll(x, DEEP, 1) + jnp.where(lane16 < DEEP, low, high)
            else:
                along_lon = pltpu.roll(x + jnp.where(lane16 < DEEP, high, low), DEEP, 1)
            deeper = jnp.where(lane16 % DEEP == 0, 0.0, pltpu.roll(x, 1, 1))
            higher = jnp.where(lane16 % DEEP == DEEP - 1, 0.0, pltpu.roll(x, 127, 1))
            below = jnp.where(has_low, row_in[n, 1, pl.ds(c, 1)], 0.0)
            above = jnp.where(has_high, row_in[n, 0, pl.ds(c, 1)], 0.0)
            north = jnp.where(row16 == 0, below, pltpu.roll(x, 1, 0))
            south = jnp.where(row16 == ROWS - 1, above, pltpu.roll(x, ROWS - 1, 0))
            around = along_lon + (north + south + deeper + higher) - 6.0 * x
            return 2.0 * x - fields[n, c] + speed * around

        def component(i, carry):
            fields[n + 2, i] = one(i, False)
            fields[n + 2, 3 + i] = one(3 + i, False) + (
                c2[1, 0:ROWS] * weights[n][0:ROWS]
            ) * fields[n + 1, i]
            fields[n + 2, 6 + i] = one(6 + i, True)
            fields[n + 2, 9 + i] = one(9 + i, True)
            return carry

        lax.fori_loop(0, 3, component, 0)
        if n + 1 < STEPS:
            halos.append(send_halo(n + 1))

    step(0)

    shrink = (OFFSETS, (-1, 0, 1), (-1, 0, 1), (0,))

    def gather_sum(k, group, own_part):
        drain(k, group, 1)
        part = own_part
        for r in range(PEERS[group]):
            part = part + slots[k, r]
        total[k] = part
        return part

    gather_sum(0, "xc", chunks[me_xc])
    post(1, "y", lambda r: total.at[0], lambda r: slots.at[1, r - 1])

    step(1)
    gather_sum(1, "y", total[0])
    post(2, "z", lambda r: total.at[1], lambda r: slots.at[2, r - 1])
    step(2)
    gathered[me_xc] = gather_sum(2, "z", total[1])
    post(3, "xc", lambda r: total.at[2], lambda r: gathered.at[me_xc])
    ref = gathered.at[pl.ds(0, 7)]
    pltpu.make_async_copy(ref, ref, group_sem.at[1, 3]).wait()

    for n in range(STEPS):
        for f in range(2):
            tile = gathered[2 * n + f]
            rec[f, 3 * n : 3 * n + 3, 0:128] = tile[0:3]
            rec[f, 3 * n : 3 * n + 3, 128:256] = tile[3:6]

    def thirds(v, hot, times):
        stack = jnp.concatenate(split3(v), axis=0)
        got = times(stack, hot)
        return got[0:16] + got[16:32] + got[32:48]

    first = first_hot[...]
    second = second_hot[...]
    gen_a = thirds(rec[0], first, dot)
    corr_b = thirds(rec[1], second, dot)
    misfit = gen_a * corr_b - obs[...]
    src = (thirds(misfit * corr_b, first, dot_t), thirds(misfit * gen_a, second, dot_t))

    speed = {p: cn[p][0] for p in OFFSETS}
    hot = depth_hot[0:128]
    now = [{} for c in range(6)]
    old = [{} for c in range(6)]
    added = []
    halves = [split2(v) for v in src]
    for k in range(STEPS):
        later = STEPS - 1 - k
        for c in range(6):
            new = advance(now[c], old[c], speed, shrink[k], lane) if k else {}
            old[c] = now[c]
            line = 3 * later + c % 3
            lhs = []
            for h in halves[c // 3]:
                mine = jnp.broadcast_to(h[line : line + 1].astype(F32), (ROUND, STATIONS))
                for p in shrink[k]:
                    lhs.append(
                        jnp.where(spot == row_id + (p + 2) * ROUND, mine, 0.0).astype(BF16)
                    )
            put = dot_t(jnp.concatenate(lhs, axis=0), hot)
            count = len(shrink[k])
            for j, p in enumerate(shrink[k]):
                both = (
                    put[j * ROUND : (j + 1) * ROUND]
                    + put[(count + j) * ROUND : (count + j + 1) * ROUND]
                )
                new[p] = new[p] + both if k else both
            now[c] = new
        added.append([now[c][0][0:ROWS] for c in range(6)])

    step(3)
    kernel = jnp.zeros((ROWS, 128), F32)
    for k in range(STEPS):
        for c in range(3):
            kernel = kernel + (fields[k + 2, 9 + c] + added[k][3 + c]) * fields[STEPS + 1 - k, c]
    for c in range(3):
        last = fields[STEPS + 1, 3 + c]
        out_corr[c, 0] = last[:, 0:DEEP]
        out_corr[c, 1] = last[:, DEEP:128]
    for c in range(6):
        last = fields[STEPS + 1, 6 + c] + added[STEPS - 1][c]
        out_adj[c, 0] = last[:, 0:DEEP]
        out_adj[c, 1] = last[:, DEEP:128]
    out_kernel[0] = kernel[:, 0:DEEP]
    out_kernel[1] = kernel[:, DEEP:128]

    for copies in [cn_copies] + halos:
        for copy, da in copies:
            if da:
                pl.when(sends(da))(copy.wait_send)
            else:
                copy.wait_send()
    for k, group in enumerate(("xc", "y", "z", "xc")):
        drain(k, group, 0)


def shards(
    gen_prev,
    gen_cur,
    corr_prev,
    corr_cur,
    adj_prev,
    adj_cur,
    courant,
    noise,
    station_owner,
    station_cell,
    pairs,
    observed,
    checkpoint,
):
    anywhere = pl.BlockSpec(memory_space=pltpu.HBM)
    vmem = pl.BlockSpec(memory_space=pltpu.VMEM)
    cn = pltpu.VMEM((2, ROUND, 128), F32)
    return pl.pallas_call(
        body,
        name="window",
        out_shape=(
            jax.ShapeDtypeStruct((3, LONG, ROWS, DEEP), F32),
            jax.ShapeDtypeStruct((6, LONG, ROWS, DEEP), F32),
            jax.ShapeDtypeStruct((LONG, ROWS, DEEP), F32),
        ),
        in_specs=[anywhere] * 12 + [pl.BlockSpec(memory_space=pltpu.SMEM)],
        out_specs=(vmem, vmem, vmem),
        scratch_shapes=[
            pltpu.VMEM((2, 12, LONG, ROWS, DEEP), F32),
            pltpu.VMEM((2, LONG, ROWS, DEEP), F32),
            pltpu.VMEM((1, STATIONS), jnp.int32),
            pltpu.VMEM((1, STATIONS), jnp.int32),
            pltpu.VMEM((2, PAIRS), jnp.int32),
            pltpu.VMEM((3, STEPS, PAIRS), F32),
            pltpu.VMEM((STEPS + 2, 12, ROWS, 128), F32),
            cn,
            cn,
            cn,
            cn,
            cn,
            pltpu.VMEM((2, 5, 2, 8, 128), F32),
            pltpu.VMEM((STEPS, 2, 6, ROWS, 128), F32),
            pltpu.VMEM((STEPS, 2, 6, ROWS, 128), F32),
            pltpu.VMEM((STEPS, 2, 16, 128), F32),
            pltpu.VMEM((STEPS, 2, 16, 128), F32),
            pltpu.VMEM((256, STATIONS), BF16),
            pltpu.VMEM((STATIONS, PAIRS), BF16),
            pltpu.VMEM((STATIONS, PAIRS), BF16),
            pltpu.VMEM((16, PAIRS), F32),
            pltpu.VMEM((8, 8, 128), F32),
            pltpu.VMEM((3, 8, 128), F32),
            pltpu.VMEM((3, 11, 8, 128), F32),
            pltpu.VMEM((8, 8, 128), F32),
            pltpu.VMEM((2, 16, STATIONS), F32),
            pltpu.SemaphoreType.DMA((12,)),
            pltpu.SemaphoreType.DMA((2, 14)),
            pltpu.SemaphoreType.DMA((STEPS, 2, 4)),
            pltpu.SemaphoreType.DMA((2, 4)),
        ],
        compiler_params=pltpu.CompilerParams(
            collective_id=0, has_side_effects=True, vmem_limit_bytes=56 * 1024 * 1024
        ),
    )(
        gen_prev,
        gen_cur,
        corr_prev,
        corr_cur,
        adj_prev,
        adj_cur,
        courant,
        noise,
        station_owner.reshape(1, STATIONS),
        station_cell.reshape(1, STATIONS),
        pairs,
        jnp.transpose(observed, (1, 0, 2)),
        checkpoint,
    )


def solution(mesh):
    field = P(None, "lon", "lat", None)
    cells = P("lon", "lat", None)
    return jax.shard_map(
        shards,
        mesh=mesh,
        in_specs=(field,) * 6 + (cells,) * 2 + (P(),) * 5,
        out_specs=(field, field, cells),
        check_vma=False,
    )
```

```python
import jax
import jax.numpy as jnp
from jax import lax
from jax.experimental import pallas as pl
from jax.experimental.pallas import tpu as pltpu
from jax.sharding import PartitionSpec as P

OMEGA = 0.7
MESH = pl.DeviceIdType.MESH
F32 = jnp.float32
BF16 = jnp.bfloat16
LONS = 192
LATS = 4
RING_Z = 12
LONG = 2
ROWS = 16
DEEP = 64
TOTAL_LON = LONS * LONG
ROUND = 24
STEPS = 4
STATIONS = 256
PAIRS = 1024
STRIPS = (-1, 0, 1)
OFFSETS = (-2, -1, 0, 1, 2)
GROUPS = ("xc", "y", "z")
PEERS = {"xc": 7, "y": 7, "z": 11}


def place():
    lon = lax.axis_index("lon")
    lat = lax.axis_index("lat")
    return lon, lat, lon // 24, lon % 24


def peer(group, r):
    lon, lat, block, inner = place()
    if group == "xc":
        t = (block % 4 * 2 + inner % 2 + r) % 8
        return ((block // 4 * 4 + t // 2) * 24 + inner // 2 * 2 + t % 2, lat)
    if group == "y":
        t = (block // 4 * 4 + lat + r) % 8
        return ((t // 4 * 4 + block % 4) * 24 + inner, t % 4)
    return (block * 24 + (inner + 2 * r) % 24, lat)


def split2(v):
    high = v.astype(BF16)
    return high, (v - high.astype(F32)).astype(BF16)


def split3(v):
    high = v.astype(BF16)
    rest = v - high.astype(F32)
    mid = rest.astype(BF16)
    return high, mid, (rest - mid.astype(F32)).astype(BF16)


def dot(a, b):
    return lax.dot_general(a, b, (((1,), (0,)), ((), ())), preferred_element_type=F32)


def dot_t(a, b):
    return lax.dot_general(a, b, (((1,), (1,)), ((), ())), preferred_element_type=F32)


def laplace(cur, p, lane):
    x = cur.get(p)
    low = cur.get(p - 1)
    high = cur.get(p + 1)
    zero = jnp.zeros((ROUND, 128), F32)
    sides = jnp.where(
        lane >= DEEP, zero if low is None else low, zero if high is None else high
    )
    if x is None:
        return pltpu.roll(sides, DEEP, 1)
    along_lon = pltpu.roll(x + sides, DEEP, 1)
    deeper = jnp.where(lane % DEEP == 0, 0.0, pltpu.roll(x, 1, 1))
    higher = jnp.where(lane % DEEP == DEEP - 1, 0.0, pltpu.roll(x, 127, 1))
    north = pltpu.roll(x, 1, 0)
    south = pltpu.roll(x, ROUND - 1, 0)
    return along_lon + (north + south + deeper + higher) - 6.0 * x


def advance(cur, old, speed, pairs, lane):
    new = {}
    for p in pairs:
        v = speed[p] * laplace(cur, p, lane)
        if p in cur:
            v = v + 2.0 * cur[p]
        if p in old:
            v = v - old[p]
        new[p] = v
    return new


def body(
    gen_prev,
    gen_cur,
    corr_prev,
    corr_cur,
    adj_prev,
    adj_cur,
    courant,
    noise,
    owner,
    cell,
    pairs,
    observed,
    checkpoint,
    out_corr,
    out_adj,
    out_kernel,
    st_fields,
    st_cn,
    v_owner,
    v_cell,
    v_pairs,
    v_obs,
    fields,
    c0,
    c1,
    c2,
    c3,
    c4,
    cn_strip,
    side_out,
    side_in,
    row_out,
    row_in,
    corner_in,
    depth_hot,
    first_hot,
    second_hot,
    obs,
    chunks,
    total,
    slots,
    gathered,
    rec,
    load_sem,
    cn_sem,
    halo_sem,
    group_sem,
):
    lon, lat, block, inner = place()
    cn = {-2: c0, -1: c1, 0: c2, 1: c3, 2: c4}
    loads = []
    sources = [
        (courant, st_cn.at[0]),
        (noise, st_cn.at[1]),
        (gen_cur, st_fields.at[0, pl.ds(0, 3)]),
        (corr_cur, st_fields.at[0, pl.ds(3, 3)]),
        (gen_prev, st_fields.at[1, pl.ds(0, 3)]),
        (corr_prev, st_fields.at[1, pl.ds(3, 3)]),
        (adj_cur, st_fields.at[0, pl.ds(6, 6)]),
        (adj_prev, st_fields.at[1, pl.ds(6, 6)]),
        (owner, v_owner),
        (cell, v_cell),
        (pairs, v_pairs),
        (observed, v_obs),
    ]
    for i, (src, dst) in enumerate(sources):
        copy = pltpu.make_async_copy(src, dst, load_sem.at[i])
        copy.start()
        loads.append(copy)
    barrier = pltpu.get_barrier_semaphore()
    greeted = 0
    for dl in OFFSETS:
        for da in STRIPS:
            if dl or da:
                pl.semaphore_signal(
                    barrier,
                    inc=1,
                    device_id=((lon + dl + LONS) % LONS, (lat + da + LATS) % LATS),
                    device_id_type=MESH,
                )
                greeted += 1
    for group in GROUPS:

        def greet(r, carry, group=group):
            pl.semaphore_signal(barrier, inc=1, device_id=peer(group, r), device_id_type=MESH)
            return carry

        lax.fori_loop(1, PEERS[group] + 1, greet, 0)
        greeted += PEERS[group]

    lane = lax.broadcasted_iota(jnp.int32, (ROUND, 128), 1)
    sub8 = lax.broadcasted_iota(jnp.int32, (8, 128), 0)
    zeros8 = jnp.zeros((8, 128), F32)

    loads[0].wait()
    loads[1].wait()
    for ch in range(2):
        c2[ch, 0:ROWS] = jnp.concatenate([st_cn[ch, 0], st_cn[ch, 1]], axis=1)
    pl.semaphore_wait(barrier, greeted)

    has_low = lat > 0
    has_high = lat < LATS - 1

    def target(dl, da):
        return ((lon + dl + LONS) % LONS, (lat + da + LATS) % LATS)

    def remote(src, dst, sems, k, dl, da):
        return pltpu.make_async_remote_copy(
            src, dst, sems.at[0, k], sems.at[1, k], device_id=target(dl, da), device_id_type=MESH
        )

    cn_copies = []
    for dl in (-1, 1, -2, 2):
        cn_copies.append(
            (
                remote(
                    c2.at[:, pl.ds(0, ROWS)],
                    cn[-dl].at[:, pl.ds(0, ROWS)],
                    cn_sem,
                    len(cn_copies),
                    dl,
                    0,
                ),
                0,
            )
        )
    for dl in (0, -1, 1, -2, 2):
        for da in (-1, 1):
            cn_copies.append(
                (
                    remote(
                        c2.at[:, pl.ds(0 if da < 0 else 8, 8)],
                        cn_strip.at[0 if da < 0 else 1, 2 - dl],
                        cn_sem,
                        len(cn_copies),
                        dl,
                        da,
                    ),
                    da,
                )
            )

    def sends(da):
        return has_low if da < 0 else has_high

    def receives(da):
        return has_high if da < 0 else has_low

    def go(copies):
        for copy, da in copies:
            if da:
                pl.when(sends(da))(copy.start)
            else:
                copy.start()

    def take(copies):
        for copy, da in copies:
            if da:
                pl.when(receives(da))(copy.wait_recv)
            else:
                copy.wait_recv()

    go(cn_copies)

    for k in range(2, 8):
        loads[k].wait()

    for ch in range(12):
        for t in range(2):
            wide = jnp.concatenate([st_fields[t, ch, 0], st_fields[t, ch, 1]], axis=1)
            fields[1 - t, ch] = wide
    lane16 = lane[0:ROWS]
    row16 = lax.broadcasted_iota(jnp.int32, (ROWS, 128), 0)

    def halo(h):
        copies = []
        for d, dl in enumerate((-1, 1)):
            copies.append(
                (remote(side_out.at[h, d], side_in.at[h, d], halo_sem.at[h], len(copies), dl, 0), 0)
            )
        for d, da in enumerate((-1, 1)):
            copies.append(
                (remote(row_out.at[h, d], row_in.at[h, d], halo_sem.at[h], len(copies), 0, da), da)
            )
        for d, da in enumerate((-1, 1)):
            for e, dl in enumerate((-1, 1)):
                copies.append(
                    (
                        remote(
                            row_out.at[h, d, 0],
                            corner_in.at[h, d, e],
                            halo_sem.at[h],
                            len(copies),
                            dl,
                            da,
                        ),
                        da,
                    )
                )
        return copies

    def turn(x):
        return pltpu.roll(x, DEEP, 1)

    def send_halo(h):
        n = 2 * h + 1
        for c in range(6):
            one, two = fields[n, c], fields[n, c + 6]
            one_t, two_t = turn(one), turn(two)
            side_out[h, 0, 0, c] = jnp.where(lane16 < DEEP, one, two_t)
            side_out[h, 1, 0, c] = jnp.where(lane16 < DEEP, two_t, one)
            side_out[h, 0, 1, c] = jnp.where(lane16 < DEEP, one_t, two)
            side_out[h, 1, 1, c] = jnp.where(lane16 < DEEP, two, one_t)
            one, two_t = fields[n - 1, c], turn(fields[n - 1, c + 6])
            side_out[h, 0, 2, c] = jnp.where(lane16 < DEEP, one, two_t)
            side_out[h, 1, 2, c] = jnp.where(lane16 < DEEP, two_t, one)
        for c in range(12):
            now, before = fields[n, c], fields[n - 1, c]
            row_out[h, 0, 0, c : c + 1] = now[0:1]
            row_out[h, 0, 1, c : c + 1] = now[1:2]
            row_out[h, 0, 2, c : c + 1] = before[0:1]
            row_out[h, 1, 0, c : c + 1] = now[ROWS - 1 : ROWS]
            row_out[h, 1, 1, c : c + 1] = now[ROWS - 2 : ROWS - 1]
            row_out[h, 1, 2, c : c + 1] = before[ROWS - 1 : ROWS]
        copies = halo(h)
        go(copies)
        return copies

    halos = [send_halo(0)]
    for k in range(8, 12):
        loads[k].wait()

    own = v_owner[...]
    where_in = v_cell[...]
    slon = own * LONG + where_in // (LATS * ROWS * DEEP)
    slat = where_in // DEEP % (LATS * ROWS)
    slane = where_in // (LATS * ROWS * DEEP) * DEEP + where_in % DEEP
    rel_lon = (slon - lon * LONG + 4 + TOTAL_LON) % TOTAL_LON
    rel_lat = slat - lat * ROWS
    near = (rel_lon < 10) & (rel_lat >= -4) & (rel_lat < ROWS + 4)
    row24 = jnp.where(rel_lat < 0, rel_lat + ROUND, rel_lat)
    spot = jnp.where(near, rel_lon // 2 * ROUND + row24, -1)
    spot = jnp.broadcast_to(spot, (ROUND, STATIONS))
    row_id = lax.broadcasted_iota(jnp.int32, (ROUND, STATIONS), 0)
    lanes = lax.broadcasted_iota(jnp.int32, (128, STATIONS), 0)
    hot = jnp.where(lanes == slane, 1.0, 0.0).astype(BF16)
    depth_hot[0:128] = hot
    depth_hot[128:256] = hot

    phase = checkpoint[0].astype(F32)
    weights = [jnp.cos(jnp.full((ROUND, 128), OMEGA * (phase + n), F32)) for n in range(STEPS)]

    ids = lax.broadcasted_iota(jnp.int32, (STATIONS, PAIRS), 0)
    first_hot[...] = jnp.where(ids == v_pairs[0:1], 1.0, 0.0).astype(BF16)
    second_hot[...] = jnp.where(ids == v_pairs[1:2], 1.0, 0.0).astype(BF16)
    rec[...] = jnp.zeros(rec.shape, F32)
    obs[...] = jnp.zeros(obs.shape, F32)
    for n in range(STEPS):
        for i in range(3):
            obs[3 * n + i : 3 * n + i + 1] = v_obs[i, n : n + 1]
    for j in range(8):
        chunks[j, 6:8] = jnp.zeros((2, 128), F32)

    take(cn_copies)
    for p in OFFSETS:
        for ch in range(2):
            above = jnp.where(has_high, cn_strip[0, p + 2, ch], zeros8)
            below = jnp.where(has_low, cn_strip[1, p + 2, ch], zeros8)
            cn[p][ch, ROWS:ROUND] = jnp.where(sub8 < 4, above, below)
    reach = ((-1, 0, 1), (-1, 0, 1), OFFSETS, OFFSETS)

    def responses(i):
        pad = jnp.zeros((8, 128), F32)

        def own_cells(t, ch):
            return jnp.concatenate([fields[1 - t, ch], pad], axis=0)

        speed = {p: cn[p][0] for p in OFFSETS}
        gen = {0: own_cells(0, i)}
        gen_old = {0: own_cells(1, i)}
        corr = {0: own_cells(0, 3 + i)}
        corr_old = {0: own_cells(1, 3 + i)}
        for n in range(STEPS):
            gen_new = advance(gen, gen_old, speed, reach[n], lane)
            corr_new = advance(corr, corr_old, speed, reach[n], lane)
            for p in reach[n]:
                if p in gen:
                    corr_new[p] = corr_new[p] + (cn[p][1] * weights[n]) * gen[p]
            gen_old, gen = gen, gen_new
            corr_old, corr = corr, corr_new
            tiles = [field[p] for field in (gen, corr) for p in reach[n]]
            stack = jnp.concatenate(tiles, axis=0)
            picked = dot(jnp.concatenate(split2(stack), axis=1), depth_hot[...])
            for f in range(2):
                summed = jnp.zeros((ROUND, STATIONS), F32)
                for k, p in enumerate(reach[n]):
                    at = (f * len(reach[n]) + k) * ROUND
                    summed = summed + jnp.where(
                        spot == row_id + (p + 2) * ROUND, picked[at : at + ROUND], 0.0
                    )
                line = jnp.sum(summed, axis=0, keepdims=True)
                chunks[2 * n + f, i : i + 1] = line[:, 0:128]
                chunks[2 * n + f, 3 + i : 4 + i] = line[:, 128:256]

    for i in range(3):
        responses(i)

    me_xc = block % 4 * 2 + inner % 2

    def post(k, group, src_of, dst_of):
        def one(r, carry):
            pltpu.make_async_remote_copy(
                src_of(r),
                dst_of(r),
                group_sem.at[0, k],
                group_sem.at[1, k],
                device_id=peer(group, r),
                device_id_type=MESH,
            ).start()
            return carry

        lax.fori_loop(1, PEERS[group] + 1, one, 0)

    def drain(k, group, side):
        ref = slots.at[k % 3, pl.ds(0, PEERS[group])]
        pltpu.make_async_copy(ref, ref, group_sem.at[side, k]).wait()

    post(0, "xc", lambda r: chunks.at[(me_xc + r) % 8], lambda r: slots.at[0, r - 1])

    def depth_sum(x, lanes):
        deeper = jnp.where(lanes % DEEP == 0, 0.0, pltpu.roll(x, 1, 1))
        higher = jnp.where(lanes % DEEP == DEEP - 1, 0.0, pltpu.roll(x, 127, 1))
        return deeper + higher

    def lat_sum(x, below, above):
        north = jnp.where(row16 == 0, below, pltpu.roll(x, 1, 0))
        south = jnp.where(row16 == ROWS - 1, above, pltpu.roll(x, ROWS - 1, 0))
        return north + south

    def step(n, sides, rows):
        speed = c2[0, 0:ROWS]
        noisy = c2[1, 0:ROWS] * weights[n][0:ROWS]
        for c in range(12):
            x = fields[n + 1, c]
            low, high = sides[0][c % 6], sides[1][c % 6]
            if c < 6:
                along_lon = turn(x + jnp.where(lane16 < DEEP, high, low))
            else:
                along_lon = turn(x) + jnp.where(lane16 < DEEP, low, high)
            near = lat_sum(x, rows[0][c : c + 1], rows[1][c : c + 1])
            around = along_lon + (near + depth_sum(x, lane16)) - 6.0 * x
            new = 2.0 * x - fields[n, c] + speed * around
            if 3 <= c < 6:
                new = new + noisy * fields[n + 1, c - 3]
            fields[n + 2, c] = new

    def layer(h):
        n = 2 * h
        arrived = (has_low, has_high)
        row = [
            [jnp.where(arrived[d], row_in[h, 1 - d, j], 0.0) for j in range(3)] for d in range(2)
        ]
        corner = [
            [jnp.where(arrived[d], corner_in[h, 1 - d, 1 - e], 0.0) for e in range(2)]
            for d in range(2)
        ]
        sides_now = [[side_in[h, 1 - e, 0, c] for c in range(6)] for e in range(2)]
        sides_new = []
        for e in range(2):
            own_half = lane16 >= DEEP if e == 0 else lane16 < DEEP
            cells = cn[-1 if e == 0 else 1]
            speed = cells[0, 0:ROWS]
            speed = jnp.where(own_half, speed, turn(speed))
            noisy = jnp.where(own_half, cells[1, 0:ROWS] * weights[n][0:ROWS], 0.0)
            ends = [
                jnp.where(own_half, corner[d][e], turn(pltpu.roll(corner[d][e], 10, 0)))
                for d in range(2)
            ]
            new = []
            for c in range(6):
                x = sides_now[e][c]
                along_lon = side_in[h, 1 - e, 1, c] + side_out[h, 1 - e, 1, c]
                near = lat_sum(x, ends[0][c : c + 1], ends[1][c : c + 1])
                around = along_lon + (near + depth_sum(x, lane16)) - 6.0 * x
                v = 2.0 * x - side_in[h, 1 - e, 2, c] + speed * around
                if c >= 3:
                    v = v + noisy * sides_now[e][c - 3]
                new.append(v)
            sides_new.append(new)
        rows_now = [row[d][0] for d in range(2)]
        rows_new = []
        for d in range(2):
            at = ROUND - 1 if d == 0 else ROWS
            x = rows_now[d]
            sides = jnp.where(lane16 < DEEP, corner[d][1], corner[d][0])
            own = row_out[h, d, 0]
            around = turn(x + sides) + (own + row[d][1] + depth_sum(x, lane16)) - 6.0 * x
            v = 2.0 * x - row[d][2] + c2[0, at : at + 1] * around
            moved = jnp.where((row16 >= 3) & (row16 < 6), pltpu.roll(x, 3, 0), 0.0)
            v = v + (c2[1, at : at + 1] * weights[n][0:1]) * moved
            rows_new.append(v)
        return (sides_now, rows_now), (sides_new, rows_new)

    def two_steps(h):
        take(halos[h])
        now, new = layer(h)
        step(2 * h, *now)
        step(2 * h + 1, *new)

    two_steps(0)
    halos.append(send_halo(1))

    shrink = (OFFSETS, (-1, 0, 1), (-1, 0, 1), (0,))

    def gather_sum(k, group, own_part):
        drain(k, group, 1)
        part = own_part
        for r in range(PEERS[group]):
            part = part + slots[k, r]
        total[k] = part
        return part

    gather_sum(0, "xc", chunks[me_xc])
    post(1, "y", lambda r: total.at[0], lambda r: slots.at[1, r - 1])

    gather_sum(1, "y", total[0])
    post(2, "z", lambda r: total.at[1], lambda r: slots.at[2, r - 1])
    two_steps(1)
    gathered[me_xc] = gather_sum(2, "z", total[1])
    post(3, "xc", lambda r: total.at[2], lambda r: gathered.at[me_xc])
    ref = gathered.at[pl.ds(0, 7)]
    pltpu.make_async_copy(ref, ref, group_sem.at[1, 3]).wait()

    for n in range(STEPS):
        for f in range(2):
            tile = gathered[2 * n + f]
            rec[f, 3 * n : 3 * n + 3, 0:128] = tile[0:3]
            rec[f, 3 * n : 3 * n + 3, 128:256] = tile[3:6]

    def thirds(v, hot, times):
        stack = jnp.concatenate(split3(v), axis=0)
        got = times(stack, hot)
        return got[0:16] + got[16:32] + got[32:48]

    first = first_hot[...]
    second = second_hot[...]
    gen_a = thirds(rec[0], first, dot)
    corr_b = thirds(rec[1], second, dot)
    misfit = gen_a * corr_b - obs[...]
    src = (thirds(misfit * corr_b, first, dot_t), thirds(misfit * gen_a, second, dot_t))

    speed = {p: cn[p][0] for p in OFFSETS}
    hot = depth_hot[0:128]
    now = [{} for c in range(6)]
    old = [{} for c in range(6)]
    added = []
    halves = [split2(v) for v in src]
    for k in range(STEPS):
        later = STEPS - 1 - k
        for c in range(6):
            new = advance(now[c], old[c], speed, shrink[k], lane) if k else {}
            old[c] = now[c]
            line = 3 * later + c % 3
            lhs = []
            for h in halves[c // 3]:
                mine = jnp.broadcast_to(h[line : line + 1].astype(F32), (ROUND, STATIONS))
                for p in shrink[k]:
                    lhs.append(
                        jnp.where(spot == row_id + (p + 2) * ROUND, mine, 0.0).astype(BF16)
                    )
            put = dot_t(jnp.concatenate(lhs, axis=0), hot)
            count = len(shrink[k])
            for j, p in enumerate(shrink[k]):
                both = (
                    put[j * ROUND : (j + 1) * ROUND]
                    + put[(count + j) * ROUND : (count + j + 1) * ROUND]
                )
                new[p] = new[p] + both if k else both
            now[c] = new
        added.append([now[c][0][0:ROWS] for c in range(6)])

    kernel = jnp.zeros((ROWS, 128), F32)
    for k in range(STEPS):
        for c in range(3):
            kernel = kernel + (fields[k + 2, 9 + c] + added[k][3 + c]) * fields[STEPS + 1 - k, c]
    for c in range(3):
        last = fields[STEPS + 1, 3 + c]
        out_corr[c, 0] = last[:, 0:DEEP]
        out_corr[c, 1] = last[:, DEEP:128]
    for c in range(6):
        last = fields[STEPS + 1, 6 + c] + added[STEPS - 1][c]
        out_adj[c, 0] = last[:, 0:DEEP]
        out_adj[c, 1] = last[:, DEEP:128]
    out_kernel[0] = kernel[:, 0:DEEP]
    out_kernel[1] = kernel[:, DEEP:128]

    for copies in [cn_copies] + halos:
        for copy, da in copies:
            if da:
                pl.when(sends(da))(copy.wait_send)
            else:
                copy.wait_send()
    for k, group in enumerate(("xc", "y", "z", "xc")):
        drain(k, group, 0)


def shards(
    gen_prev,
    gen_cur,
    corr_prev,
    corr_cur,
    adj_prev,
    adj_cur,
    courant,
    noise,
    station_owner,
    station_cell,
    pairs,
    observed,
    checkpoint,
):
    anywhere = pl.BlockSpec(memory_space=pltpu.HBM)
    vmem = pl.BlockSpec(memory_space=pltpu.VMEM)
    cn = pltpu.VMEM((2, ROUND, 128), F32)
    return pl.pallas_call(
        body,
        name="window",
        out_shape=(
            jax.ShapeDtypeStruct((3, LONG, ROWS, DEEP), F32),
            jax.ShapeDtypeStruct((6, LONG, ROWS, DEEP), F32),
            jax.ShapeDtypeStruct((LONG, ROWS, DEEP), F32),
        ),
        in_specs=[anywhere] * 12 + [pl.BlockSpec(memory_space=pltpu.SMEM)],
        out_specs=(vmem, vmem, vmem),
        scratch_shapes=[
            pltpu.VMEM((2, 12, LONG, ROWS, DEEP), F32),
            pltpu.VMEM((2, LONG, ROWS, DEEP), F32),
            pltpu.VMEM((1, STATIONS), jnp.int32),
            pltpu.VMEM((1, STATIONS), jnp.int32),
            pltpu.VMEM((2, PAIRS), jnp.int32),
            pltpu.VMEM((3, STEPS, PAIRS), F32),
            pltpu.VMEM((STEPS + 2, 12, ROWS, 128), F32),
            cn,
            cn,
            cn,
            cn,
            cn,
            pltpu.VMEM((2, 5, 2, 8, 128), F32),
            pltpu.VMEM((2, 2, 3, 6, ROWS, 128), F32),
            pltpu.VMEM((2, 2, 3, 6, ROWS, 128), F32),
            pltpu.VMEM((2, 2, 3, 16, 128), F32),
            pltpu.VMEM((2, 2, 3, 16, 128), F32),
            pltpu.VMEM((2, 2, 2, 16, 128), F32),
            pltpu.VMEM((256, STATIONS), BF16),
            pltpu.VMEM((STATIONS, PAIRS), BF16),
            pltpu.VMEM((STATIONS, PAIRS), BF16),
            pltpu.VMEM((16, PAIRS), F32),
            pltpu.VMEM((8, 8, 128), F32),
            pltpu.VMEM((3, 8, 128), F32),
            pltpu.VMEM((3, 11, 8, 128), F32),
            pltpu.VMEM((8, 8, 128), F32),
            pltpu.VMEM((2, 16, STATIONS), F32),
            pltpu.SemaphoreType.DMA((12,)),
            pltpu.SemaphoreType.DMA((2, 14)),
            pltpu.SemaphoreType.DMA((2, 2, 8)),
            pltpu.SemaphoreType.DMA((2, 4)),
        ],
        compiler_params=pltpu.CompilerParams(
            collective_id=0, has_side_effects=True, vmem_limit_bytes=56 * 1024 * 1024
        ),
    )(
        gen_prev,
        gen_cur,
        corr_prev,
        corr_cur,
        adj_prev,
        adj_cur,
        courant,
        noise,
        station_owner.reshape(1, STATIONS),
        station_cell.reshape(1, STATIONS),
        pairs,
        jnp.transpose(observed, (1, 0, 2)),
        checkpoint,
    )


def solution(mesh):
    field = P(None, "lon", "lat", None)
    cells = P("lon", "lat", None)
    return jax.shard_map(
        shards,
        mesh=mesh,
        in_specs=(field,) * 6 + (cells,) * 2 + (P(),) * 5,
        out_specs=(field, field, cells),
        check_vma=False,
    )
```

```python
import jax
import jax.numpy as jnp
from jax import lax
from jax.experimental import pallas as pl
from jax.experimental.pallas import tpu as pltpu
from jax.sharding import PartitionSpec as P

OMEGA = 0.7
MESH = pl.DeviceIdType.MESH
F32 = jnp.float32
BF16 = jnp.bfloat16
LONS = 192
LATS = 4
RING_Z = 12
LONG = 2
ROWS = 16
DEEP = 64
TOTAL_LON = LONS * LONG
ROUND = 24
STEPS = 4
STATIONS = 256
PAIRS = 1024
STRIPS = (-1, 0, 1)
OFFSETS = (-2, -1, 0, 1, 2)
SPREAD = (
    ((0, 24), (-1, 24), (1, 24), (-2, 16), (2, 16)),
    ((0, 24), (-1, 24), (1, 24)),
    ((0, 24), (-1, 16), (1, 16)),
    ((0, 16),),
)
GROUPS = ("xc", "y", "z")
PEERS = {"xc": 7, "y": 7, "z": 11}


def place():
    lon = lax.axis_index("lon")
    lat = lax.axis_index("lat")
    return lon, lat, lon // 24, lon % 24


def peer(group, r):
    lon, lat, block, inner = place()
    if group == "xc":
        t = (block % 4 * 2 + inner % 2 + r) % 8
        return ((block // 4 * 4 + t // 2) * 24 + inner // 2 * 2 + t % 2, lat)
    if group == "y":
        t = (block // 4 * 4 + lat + r) % 8
        return ((t // 4 * 4 + block % 4) * 24 + inner, t % 4)
    return (block * 24 + (inner + 2 * r) % 24, lat)


def split2(v):
    high = v.astype(BF16)
    return high, (v - high.astype(F32)).astype(BF16)


def split3(v):
    high = v.astype(BF16)
    rest = v - high.astype(F32)
    mid = rest.astype(BF16)
    return high, mid, (rest - mid.astype(F32)).astype(BF16)


def dot(a, b):
    return lax.dot_general(a, b, (((1,), (0,)), ((), ())), preferred_element_type=F32)


def dot_t(a, b):
    return lax.dot_general(a, b, (((1,), (1,)), ((), ())), preferred_element_type=F32)


def laplace(cur, p, lane):
    x = cur.get(p)
    low = cur.get(p - 1)
    high = cur.get(p + 1)
    zero = jnp.zeros((ROUND, 128), F32)
    sides = jnp.where(
        lane >= DEEP, zero if low is None else low, zero if high is None else high
    )
    if x is None:
        return pltpu.roll(sides, DEEP, 1)
    along_lon = pltpu.roll(x + sides, DEEP, 1)
    deeper = jnp.where(lane % DEEP == 0, 0.0, pltpu.roll(x, 1, 1))
    higher = jnp.where(lane % DEEP == DEEP - 1, 0.0, pltpu.roll(x, 127, 1))
    north = pltpu.roll(x, 1, 0)
    south = pltpu.roll(x, ROUND - 1, 0)
    return along_lon + (north + south + deeper + higher) - 6.0 * x


def advance(cur, old, speed, pairs, lane):
    new = {}
    for p in pairs:
        v = speed[p] * laplace(cur, p, lane)
        if p in cur:
            v = v + 2.0 * cur[p]
        if p in old:
            v = v - old[p]
        new[p] = v
    return new


def body(
    gen_prev,
    gen_cur,
    corr_prev,
    corr_cur,
    adj_prev,
    adj_cur,
    courant,
    noise,
    owner,
    cell,
    pairs,
    observed,
    checkpoint,
    out_corr,
    out_adj,
    out_kernel,
    st_fields,
    st_cn,
    v_owner,
    v_cell,
    v_pairs,
    v_obs,
    fields,
    c0,
    c1,
    c2,
    c3,
    c4,
    cn_strip,
    side_out,
    side_in,
    row_out,
    row_in,
    corner_in,
    place_hot,
    depth_hot,
    first_hot,
    second_hot,
    obs,
    chunks,
    total,
    slots,
    gathered,
    rec,
    load_sem,
    cn_sem,
    halo_sem,
    group_sem,
):
    lon, lat, block, inner = place()
    cn = {-2: c0, -1: c1, 0: c2, 1: c3, 2: c4}
    barrier = pltpu.get_barrier_semaphore()
    greeted = 0
    for dl in OFFSETS:
        for da in STRIPS:
            if dl or da:
                pl.semaphore_signal(
                    barrier,
                    inc=1,
                    device_id=((lon + dl + LONS) % LONS, (lat + da + LATS) % LATS),
                    device_id_type=MESH,
                )
                greeted += 1
    loads = []
    sources = [
        (courant, st_cn.at[0]),
        (noise, st_cn.at[1]),
        (gen_cur, st_fields.at[0, pl.ds(0, 3)]),
        (corr_cur, st_fields.at[0, pl.ds(3, 3)]),
        (gen_prev, st_fields.at[1, pl.ds(0, 3)]),
        (corr_prev, st_fields.at[1, pl.ds(3, 3)]),
        (adj_cur, st_fields.at[0, pl.ds(6, 6)]),
        (adj_prev, st_fields.at[1, pl.ds(6, 6)]),
        (owner, v_owner),
        (cell, v_cell),
        (pairs, v_pairs),
        (observed, v_obs),
    ]
    for i, (src, dst) in enumerate(sources):
        copy = pltpu.make_async_copy(src, dst, load_sem.at[i])
        copy.start()
        loads.append(copy)
    for group in GROUPS:

        def greet(r, carry, group=group):
            pl.semaphore_signal(barrier, inc=1, device_id=peer(group, r), device_id_type=MESH)
            return carry

        lax.fori_loop(1, PEERS[group] + 1, greet, 0, unroll=True)
        greeted += PEERS[group]

    lane = lax.broadcasted_iota(jnp.int32, (ROUND, 128), 1)
    sub8 = lax.broadcasted_iota(jnp.int32, (8, 128), 0)
    zeros8 = jnp.zeros((8, 128), F32)

    loads[0].wait()
    loads[1].wait()
    for ch in range(2):
        c2[ch, 0:ROWS] = jnp.concatenate([st_cn[ch, 0], st_cn[ch, 1]], axis=1)
    pl.semaphore_wait(barrier, greeted)

    has_low = lat > 0
    has_high = lat < LATS - 1

    def target(dl, da):
        return ((lon + dl + LONS) % LONS, (lat + da + LATS) % LATS)

    def remote(src, dst, sems, k, dl, da):
        return pltpu.make_async_remote_copy(
            src, dst, sems.at[0, k], sems.at[1, k], device_id=target(dl, da), device_id_type=MESH
        )

    cn_copies = []
    for dl in (-1, 1, -2, 2):
        cn_copies.append(
            (
                remote(
                    c2.at[:, pl.ds(0, ROWS)],
                    cn[-dl].at[:, pl.ds(0, ROWS)],
                    cn_sem,
                    len(cn_copies),
                    dl,
                    0,
                ),
                0,
            )
        )
    for dl in (0, -1, 1, -2, 2):
        for da in (-1, 1):
            cn_copies.append(
                (
                    remote(
                        c2.at[:, pl.ds(0 if da < 0 else 8, 8)],
                        cn_strip.at[0 if da < 0 else 1, 2 - dl],
                        cn_sem,
                        len(cn_copies),
                        dl,
                        da,
                    ),
                    da,
                )
            )

    def sends(da):
        return has_low if da < 0 else has_high

    def receives(da):
        return has_high if da < 0 else has_low

    def go(copies):
        for copy, da in copies:
            if da:
                pl.when(sends(da))(copy.start)
            else:
                copy.start()

    def take(copies):
        for copy, da in copies:
            if da:
                pl.when(receives(da))(copy.wait_recv)
            else:
                copy.wait_recv()

    go(cn_copies)

    for k in range(2, 8):
        loads[k].wait()

    for ch in range(12):
        for t in range(2):
            wide = jnp.concatenate([st_fields[t, ch, 0], st_fields[t, ch, 1]], axis=1)
            fields[1 - t, ch] = wide
    lane16 = lane[0:ROWS]
    row16 = lax.broadcasted_iota(jnp.int32, (ROWS, 128), 0)

    def halo(h):
        copies = []
        for d, dl in enumerate((-1, 1)):
            copies.append(
                (remote(side_out.at[h, d], side_in.at[h, d], halo_sem.at[h], len(copies), dl, 0), 0)
            )
        for d, da in enumerate((-1, 1)):
            copies.append(
                (remote(row_out.at[h, d], row_in.at[h, d], halo_sem.at[h], len(copies), 0, da), da)
            )
        for d, da in enumerate((-1, 1)):
            for e, dl in enumerate((-1, 1)):
                copies.append(
                    (
                        remote(
                            row_out.at[h, d, 0],
                            corner_in.at[h, d, e],
                            halo_sem.at[h],
                            len(copies),
                            dl,
                            da,
                        ),
                        da,
                    )
                )
        return copies

    def turn(x):
        return pltpu.roll(x, DEEP, 1)

    def send_halo(h):
        n = 2 * h + 1
        for c in range(6):
            one, two = fields[n, c], fields[n, c + 6]
            one_t, two_t = turn(one), turn(two)
            side_out[h, 0, 0, c] = jnp.where(lane16 < DEEP, one, two_t)
            side_out[h, 1, 0, c] = jnp.where(lane16 < DEEP, two_t, one)
            side_out[h, 0, 1, c] = jnp.where(lane16 < DEEP, one_t, two)
            side_out[h, 1, 1, c] = jnp.where(lane16 < DEEP, two, one_t)
            one, two_t = fields[n - 1, c], turn(fields[n - 1, c + 6])
            side_out[h, 0, 2, c] = jnp.where(lane16 < DEEP, one, two_t)
            side_out[h, 1, 2, c] = jnp.where(lane16 < DEEP, two_t, one)
        for c in range(12):
            now, before = fields[n, c], fields[n - 1, c]
            row_out[h, 0, 0, c : c + 1] = now[0:1]
            row_out[h, 0, 1, c : c + 1] = now[1:2]
            row_out[h, 0, 2, c : c + 1] = before[0:1]
            row_out[h, 1, 0, c : c + 1] = now[ROWS - 1 : ROWS]
            row_out[h, 1, 1, c : c + 1] = now[ROWS - 2 : ROWS - 1]
            row_out[h, 1, 2, c : c + 1] = before[ROWS - 1 : ROWS]
        copies = halo(h)
        go(copies)
        return copies

    halos = [send_halo(0)]
    for k in range(8, 12):
        loads[k].wait()

    own = v_owner[...]
    where_in = v_cell[...]
    slon = own * LONG + where_in // (LATS * ROWS * DEEP)
    slat = where_in // DEEP % (LATS * ROWS)
    slane = where_in // (LATS * ROWS * DEEP) * DEEP + where_in % DEEP
    rel_lon = (slon - lon * LONG + 4 + TOTAL_LON) % TOTAL_LON
    rel_lat = slat - lat * ROWS
    near = (rel_lon < 10) & (rel_lat >= -4) & (rel_lat < ROWS + 4)
    row24 = jnp.where(rel_lat < 0, rel_lat + ROUND, rel_lat)
    spot = jnp.where(near, rel_lon // 2 * ROUND + row24, -1)
    spot = jnp.broadcast_to(spot, (ROUND, STATIONS))
    row_id = lax.broadcasted_iota(jnp.int32, (ROUND, STATIONS), 0)
    lanes = lax.broadcasted_iota(jnp.int32, (128, STATIONS), 0)
    hot = jnp.where(lanes == slane, 1.0, 0.0).astype(BF16)
    depth_hot[0:128] = hot
    depth_hot[128:256] = hot

    phase = checkpoint[0].astype(F32)
    weights = [jnp.cos(jnp.full((ROUND, 128), OMEGA * (phase + n), F32)) for n in range(STEPS)]

    ids = lax.broadcasted_iota(jnp.int32, (STATIONS, PAIRS), 0)
    first_hot[...] = jnp.where(ids == v_pairs[0:1], 1.0, 0.0).astype(BF16)
    second_hot[...] = jnp.where(ids == v_pairs[1:2], 1.0, 0.0).astype(BF16)
    rec[...] = jnp.zeros(rec.shape, F32)
    obs[...] = jnp.zeros(obs.shape, F32)
    for n in range(STEPS):
        for i in range(3):
            obs[3 * n + i : 3 * n + i + 1] = v_obs[i, n : n + 1]
    for p in OFFSETS:
        place_hot[p + 2] = jnp.where(spot == row_id + (p + 2) * ROUND, 1.0, 0.0)
    for j in range(8):
        chunks[j, 6:8] = jnp.zeros((2, 128), F32)

    take(cn_copies)
    for p in OFFSETS:
        for ch in range(2):
            above = jnp.where(has_high, cn_strip[0, p + 2, ch], zeros8)
            below = jnp.where(has_low, cn_strip[1, p + 2, ch], zeros8)
            cn[p][ch, ROWS:ROUND] = jnp.where(sub8 < 4, above, below)
    reach = ((-1, 0, 1), (-1, 0, 1), OFFSETS, OFFSETS)

    def responses(i):
        pad = jnp.zeros((8, 128), F32)

        def own_cells(t, ch):
            return jnp.concatenate([fields[1 - t, ch], pad], axis=0)

        speed = {p: cn[p][0] for p in OFFSETS}
        gen = {0: own_cells(0, i)}
        gen_old = {0: own_cells(1, i)}
        corr = {0: own_cells(0, 3 + i)}
        corr_old = {0: own_cells(1, 3 + i)}
        for n in range(STEPS):
            gen_new = advance(gen, gen_old, speed, reach[n], lane)
            corr_new = advance(corr, corr_old, speed, reach[n], lane)
            for p in reach[n]:
                if p in gen:
                    corr_new[p] = corr_new[p] + (cn[p][1] * weights[n]) * gen[p]
            gen_old, gen = gen, gen_new
            corr_old, corr = corr, corr_new
            tiles = [field[p] for field in (gen, corr) for p in reach[n]]
            stack = jnp.concatenate(tiles, axis=0)
            picked = dot(jnp.concatenate(split2(stack), axis=1), depth_hot[...])
            for f in range(2):
                summed = jnp.zeros((ROUND, STATIONS), F32)
                for k, p in enumerate(reach[n]):
                    at = (f * len(reach[n]) + k) * ROUND
                    summed = summed + place_hot[p + 2] * picked[at : at + ROUND]
                line = jnp.sum(summed, axis=0, keepdims=True)
                chunks[2 * n + f, i : i + 1] = line[:, 0:128]
                chunks[2 * n + f, 3 + i : 4 + i] = line[:, 128:256]

    for i in range(3):
        responses(i)

    me_xc = block % 4 * 2 + inner % 2

    def post(k, group, src_of, dst_of):
        def one(r, carry):
            pltpu.make_async_remote_copy(
                src_of(r),
                dst_of(r),
                group_sem.at[0, k],
                group_sem.at[1, k],
                device_id=peer(group, r),
                device_id_type=MESH,
            ).start()
            return carry

        lax.fori_loop(1, PEERS[group] + 1, one, 0, unroll=True)

    def drain(k, group, side):
        ref = slots.at[k % 3, pl.ds(0, PEERS[group])]
        pltpu.make_async_copy(ref, ref, group_sem.at[side, k]).wait()

    post(0, "xc", lambda r: chunks.at[(me_xc + r) % 8], lambda r: slots.at[0, r - 1])

    def depth_sum(x, lanes):
        deeper = jnp.where(lanes % DEEP == 0, 0.0, pltpu.roll(x, 1, 1))
        higher = jnp.where(lanes % DEEP == DEEP - 1, 0.0, pltpu.roll(x, 127, 1))
        return deeper + higher

    def lat_sum(x, below, above):
        north = jnp.where(row16 == 0, below, pltpu.roll(x, 1, 0))
        south = jnp.where(row16 == ROWS - 1, above, pltpu.roll(x, ROWS - 1, 0))
        return north + south

    def step(n, sides, rows):
        speed = c2[0, 0:ROWS]
        noisy = c2[1, 0:ROWS] * weights[n][0:ROWS]
        for c in range(12):
            x = fields[n + 1, c]
            low, high = sides[0][c % 6], sides[1][c % 6]
            if c < 6:
                along_lon = turn(x + jnp.where(lane16 < DEEP, high, low))
            else:
                along_lon = turn(x) + jnp.where(lane16 < DEEP, low, high)
            near = lat_sum(x, rows[0][c : c + 1], rows[1][c : c + 1])
            around = along_lon + (near + depth_sum(x, lane16)) - 6.0 * x
            new = 2.0 * x - fields[n, c] + speed * around
            if 3 <= c < 6:
                new = new + noisy * fields[n + 1, c - 3]
            fields[n + 2, c] = new

    def layer(h):
        n = 2 * h
        arrived = (has_low, has_high)
        row = [
            [jnp.where(arrived[d], row_in[h, 1 - d, j], 0.0) for j in range(3)] for d in range(2)
        ]
        corner = [
            [jnp.where(arrived[d], corner_in[h, 1 - d, 1 - e], 0.0) for e in range(2)]
            for d in range(2)
        ]
        sides_now = [[side_in[h, 1 - e, 0, c] for c in range(6)] for e in range(2)]
        sides_new = []
        for e in range(2):
            own_half = lane16 >= DEEP if e == 0 else lane16 < DEEP
            cells = cn[-1 if e == 0 else 1]
            speed = cells[0, 0:ROWS]
            speed = jnp.where(own_half, speed, turn(speed))
            noisy = jnp.where(own_half, cells[1, 0:ROWS] * weights[n][0:ROWS], 0.0)
            ends = [
                jnp.where(own_half, corner[d][e], turn(pltpu.roll(corner[d][e], 10, 0)))
                for d in range(2)
            ]
            new = []
            for c in range(6):
                x = sides_now[e][c]
                along_lon = side_in[h, 1 - e, 1, c] + side_out[h, 1 - e, 1, c]
                near = lat_sum(x, ends[0][c : c + 1], ends[1][c : c + 1])
                around = along_lon + (near + depth_sum(x, lane16)) - 6.0 * x
                v = 2.0 * x - side_in[h, 1 - e, 2, c] + speed * around
                if c >= 3:
                    v = v + noisy * sides_now[e][c - 3]
                new.append(v)
            sides_new.append(new)
        rows_now = [row[d][0] for d in range(2)]
        rows_new = []
        for d in range(2):
            at = ROUND - 1 if d == 0 else ROWS
            x = rows_now[d]
            sides = jnp.where(lane16 < DEEP, corner[d][1], corner[d][0])
            own = row_out[h, d, 0]
            around = turn(x + sides) + (own + row[d][1] + depth_sum(x, lane16)) - 6.0 * x
            v = 2.0 * x - row[d][2] + c2[0, at : at + 1] * around
            moved = jnp.where((row16 >= 3) & (row16 < 6), pltpu.roll(x, 3, 0), 0.0)
            v = v + (c2[1, at : at + 1] * weights[n][0:1]) * moved
            rows_new.append(v)
        return (sides_now, rows_now), (sides_new, rows_new)

    def two_steps(h):
        take(halos[h])
        now, new = layer(h)
        step(2 * h, *now)
        step(2 * h + 1, *new)

    shrink = (OFFSETS, (-1, 0, 1), (-1, 0, 1), (0,))

    def gather_sum(k, group, own_part):
        drain(k, group, 1)
        part = own_part
        for r in range(PEERS[group]):
            part = part + slots[k, r]
        total[k] = part
        return part

    gather_sum(0, "xc", chunks[me_xc])
    post(1, "y", lambda r: total.at[0], lambda r: slots.at[1, r - 1])

    two_steps(0)
    halos.append(send_halo(1))
    gather_sum(1, "y", total[0])
    post(2, "z", lambda r: total.at[1], lambda r: slots.at[2, r - 1])
    gathered[me_xc] = gather_sum(2, "z", total[1])
    post(3, "xc", lambda r: total.at[2], lambda r: gathered.at[me_xc])
    two_steps(1)
    ref = gathered.at[pl.ds(0, 7)]
    pltpu.make_async_copy(ref, ref, group_sem.at[1, 3]).wait()

    for n in range(STEPS):
        for f in range(2):
            tile = gathered[2 * n + f]
            rec[f, 3 * n : 3 * n + 3, 0:128] = tile[0:3]
            rec[f, 3 * n : 3 * n + 3, 128:256] = tile[3:6]

    def thirds(v, hot, times):
        stack = jnp.concatenate(split3(v), axis=0)
        got = times(stack, hot)
        return got[0:16] + got[16:32] + got[32:48]

    first = first_hot[...]
    second = second_hot[...]
    gen_a = thirds(rec[0], first, dot)
    corr_b = thirds(rec[1], second, dot)
    misfit = gen_a * corr_b - obs[...]
    src = (thirds(misfit * corr_b, first, dot_t), thirds(misfit * gen_a, second, dot_t))

    speed = {p: cn[p][0] for p in OFFSETS}
    hot = depth_hot[0:128]
    now = [{} for c in range(6)]
    old = [{} for c in range(6)]
    added = []
    halves = [[h.astype(F32) for h in split2(v)] for v in src]
    for k in range(STEPS):
        later = STEPS - 1 - k
        for c in range(6):
            new = advance(now[c], old[c], speed, shrink[k], lane) if k else {}
            old[c] = now[c]
            line = 3 * later + c % 3
            parts = []
            for h in halves[c // 3]:
                mine = jnp.broadcast_to(h[line : line + 1], (ROUND, STATIONS))
                for p, rows in SPREAD[k]:
                    parts.append(place_hot[p + 2, 0:rows] * mine[0:rows])
            put = dot_t(jnp.concatenate(parts, axis=0).astype(BF16), hot)
            half = put.shape[0] // 2
            both = put[0:half] + put[half:]
            at = 0
            for p, rows in SPREAD[k]:
                piece = both[at : at + rows]
                if rows < ROUND:
                    piece = jnp.concatenate([piece, jnp.zeros((ROUND - rows, 128), F32)], axis=0)
                new[p] = new[p] + piece if k else piece
                at += rows
            now[c] = new
        added.append([now[c][0][0:ROWS] for c in range(6)])

    kernel = jnp.zeros((ROWS, 128), F32)
    for k in range(STEPS):
        for c in range(3):
            kernel = kernel + (fields[k + 2, 9 + c] + added[k][3 + c]) * fields[STEPS + 1 - k, c]
    for c in range(3):
        last = fields[STEPS + 1, 3 + c]
        out_corr[c, 0] = last[:, 0:DEEP]
        out_corr[c, 1] = last[:, DEEP:128]
    for c in range(6):
        last = fields[STEPS + 1, 6 + c] + added[STEPS - 1][c]
        out_adj[c, 0] = last[:, 0:DEEP]
        out_adj[c, 1] = last[:, DEEP:128]
    out_kernel[0] = kernel[:, 0:DEEP]
    out_kernel[1] = kernel[:, DEEP:128]

    for copies in [cn_copies] + halos:
        for copy, da in copies:
            if da:
                pl.when(sends(da))(copy.wait_send)
            else:
                copy.wait_send()
    for k, group in enumerate(("xc", "y", "z", "xc")):
        drain(k, group, 0)


def hand_over(corr, adj, kernel, out_corr, out_adj, out_kernel):
    out_corr[...] = corr[...]
    out_adj[...] = adj[...]
    out_kernel[...] = kernel[...]


def shards(
    gen_prev,
    gen_cur,
    corr_prev,
    corr_cur,
    adj_prev,
    adj_cur,
    courant,
    noise,
    station_owner,
    station_cell,
    pairs,
    observed,
    checkpoint,
):
    anywhere = pl.BlockSpec(memory_space=pltpu.HBM)
    vmem = pl.BlockSpec(memory_space=pltpu.VMEM)
    cn = pltpu.VMEM((2, ROUND, 128), F32)
    results = pl.pallas_call(
        body,
        name="window",
        out_shape=(
            jax.ShapeDtypeStruct((3, LONG, ROWS, DEEP), F32),
            jax.ShapeDtypeStruct((6, LONG, ROWS, DEEP), F32),
            jax.ShapeDtypeStruct((LONG, ROWS, DEEP), F32),
        ),
        in_specs=[anywhere] * 12 + [pl.BlockSpec(memory_space=pltpu.SMEM)],
        out_specs=(vmem, vmem, vmem),
        scratch_shapes=[
            pltpu.VMEM((2, 12, LONG, ROWS, DEEP), F32),
            pltpu.VMEM((2, LONG, ROWS, DEEP), F32),
            pltpu.VMEM((1, STATIONS), jnp.int32),
            pltpu.VMEM((1, STATIONS), jnp.int32),
            pltpu.VMEM((2, PAIRS), jnp.int32),
            pltpu.VMEM((3, STEPS, PAIRS), F32),
            pltpu.VMEM((STEPS + 2, 12, ROWS, 128), F32),
            cn,
            cn,
            cn,
            cn,
            cn,
            pltpu.VMEM((2, 5, 2, 8, 128), F32),
            pltpu.VMEM((2, 2, 3, 6, ROWS, 128), F32),
            pltpu.VMEM((2, 2, 3, 6, ROWS, 128), F32),
            pltpu.VMEM((2, 2, 3, 16, 128), F32),
            pltpu.VMEM((2, 2, 3, 16, 128), F32),
            pltpu.VMEM((2, 2, 2, 16, 128), F32),
            pltpu.VMEM((5, ROUND, STATIONS), F32),
            pltpu.VMEM((256, STATIONS), BF16),
            pltpu.VMEM((STATIONS, PAIRS), BF16),
            pltpu.VMEM((STATIONS, PAIRS), BF16),
            pltpu.VMEM((16, PAIRS), F32),
            pltpu.VMEM((8, 8, 128), F32),
            pltpu.VMEM((3, 8, 128), F32),
            pltpu.VMEM((3, 11, 8, 128), F32),
            pltpu.VMEM((8, 8, 128), F32),
            pltpu.VMEM((2, 16, STATIONS), F32),
            pltpu.SemaphoreType.DMA((12,)),
            pltpu.SemaphoreType.DMA((2, 14)),
            pltpu.SemaphoreType.DMA((2, 2, 8)),
            pltpu.SemaphoreType.DMA((2, 4)),
        ],
        compiler_params=pltpu.CompilerParams(
            collective_id=0, has_side_effects=True, vmem_limit_bytes=56 * 1024 * 1024
        ),
    )(
        gen_prev,
        gen_cur,
        corr_prev,
        corr_cur,
        adj_prev,
        adj_cur,
        courant,
        noise,
        station_owner.reshape(1, STATIONS),
        station_cell.reshape(1, STATIONS),
        pairs,
        jnp.transpose(observed, (1, 0, 2)),
        checkpoint,
    )
    return pl.pallas_call(
        hand_over,
        name="results",
        out_shape=tuple(jax.ShapeDtypeStruct(r.shape, r.dtype) for r in results),
        in_specs=[vmem] * 3,
        out_specs=(vmem,) * 3,
        compiler_params=pltpu.CompilerParams(vmem_limit_bytes=56 * 1024 * 1024),
    )(*results)


def solution(mesh):
    field = P(None, "lon", "lat", None)
    cells = P("lon", "lat", None)
    return jax.shard_map(
        shards,
        mesh=mesh,
        in_specs=(field,) * 6 + (cells,) * 2 + (P(),) * 5,
        out_specs=(field, field, cells),
        check_vma=False,
    )
```

```python
import jax
import jax.numpy as jnp
from jax import lax
from jax.experimental import pallas as pl
from jax.experimental.pallas import tpu as pltpu
from jax.sharding import PartitionSpec as P

OMEGA = 0.7
MESH = pl.DeviceIdType.MESH
F32 = jnp.float32
BF16 = jnp.bfloat16
LONS = 192
LATS = 4
RING_Z = 12
LONG = 2
ROWS = 16
DEEP = 64
TOTAL_LON = LONS * LONG
ROUND = 24
STEPS = 4
STATIONS = 256
PAIRS = 1024
STRIPS = (-1, 0, 1)
OFFSETS = (-2, -1, 0, 1, 2)
SPREAD = (
    ((0, 24), (-1, 24), (1, 24), (-2, 16), (2, 16)),
    ((0, 24), (-1, 24), (1, 24)),
    ((0, 24), (-1, 16), (1, 16)),
    ((0, 16),),
)
GROUPS = ("z", "y", "xc")
PEERS = {"xc": 7, "y": 7, "z": 11}
ORDER = {
    "xc": (4, 3, 5, 2, 6, 1, 7),
    "y": (4, 3, 5, 2, 6, 1, 7),
    "z": (6, 5, 7, 4, 8, 3, 9, 2, 10, 1, 11),
}


def place():
    lon = lax.axis_index("lon")
    lat = lax.axis_index("lat")
    return lon, lat, lon // 24, lon % 24


def peer(group, r):
    lon, lat, block, inner = place()
    if group == "xc":
        t = (block % 4 * 2 + inner % 2 + r) % 8
        return ((block // 4 * 4 + t // 2) * 24 + inner // 2 * 2 + t % 2, lat)
    if group == "y":
        t = (block // 4 * 4 + lat + r) % 8
        return ((t // 4 * 4 + block % 4) * 24 + inner, t % 4)
    return (block * 24 + (inner + 2 * r) % 24, lat)


def split2(v):
    high = v.astype(BF16)
    return high, (v - high.astype(F32)).astype(BF16)


def split3(v):
    high = v.astype(BF16)
    rest = v - high.astype(F32)
    mid = rest.astype(BF16)
    return high, mid, (rest - mid.astype(F32)).astype(BF16)


def dot(a, b):
    return lax.dot_general(a, b, (((1,), (0,)), ((), ())), preferred_element_type=F32)


def dot_t(a, b):
    return lax.dot_general(a, b, (((1,), (1,)), ((), ())), preferred_element_type=F32)


def around(cur, p, lane):
    x = cur.get(p)
    low = cur.get(p - 1)
    high = cur.get(p + 1)
    zero = jnp.zeros((ROUND, 128), F32)
    sides = jnp.where(
        lane >= DEEP, zero if low is None else low, zero if high is None else high
    )
    if x is None:
        return pltpu.roll(sides, DEEP, 1)
    along_lon = pltpu.roll(x + sides, DEEP, 1)
    deeper = jnp.where(lane % DEEP == 0, 0.0, pltpu.roll(x, 1, 1))
    higher = jnp.where(lane % DEEP == DEEP - 1, 0.0, pltpu.roll(x, 127, 1))
    north = pltpu.roll(x, 1, 0)
    south = pltpu.roll(x, ROUND - 1, 0)
    return along_lon + (north + south + deeper + higher)


def advance(cur, old, speed, hold, pairs, lane):
    new = {}
    for p in pairs:
        v = speed[p] * around(cur, p, lane)
        if p in cur:
            v = v + hold[p] * cur[p]
        if p in old:
            v = v - old[p]
        new[p] = v
    return new


def body(
    gen_prev,
    gen_cur,
    corr_prev,
    corr_cur,
    adj_prev,
    adj_cur,
    courant,
    noise,
    owner,
    cell,
    pairs,
    observed,
    checkpoint,
    out_corr,
    out_adj,
    out_kernel,
    st_fields,
    st_cn,
    v_owner,
    v_cell,
    v_pairs,
    v_obs,
    fields,
    c0,
    c1,
    c2,
    c3,
    c4,
    cn_strip,
    side_out,
    side_in,
    row_out,
    row_in,
    corner_in,
    place_hot,
    depth_hot,
    first_hot,
    second_hot,
    obs,
    chunks,
    total,
    slots,
    gathered,
    rec,
    load_sem,
    cn_sem,
    halo_sem,
    group_sem,
):
    lon, lat, block, inner = place()
    cn = {-2: c0, -1: c1, 0: c2, 1: c3, 2: c4}
    barrier = pltpu.get_barrier_semaphore()
    greeted = 0
    for dl in OFFSETS:
        for da in STRIPS:
            if dl or da:
                pl.semaphore_signal(
                    barrier,
                    inc=1,
                    device_id=((lon + dl + LONS) % LONS, (lat + da + LATS) % LATS),
                    device_id_type=MESH,
                )
                greeted += 1
    for group in GROUPS:
        for r in ORDER[group]:
            pl.semaphore_signal(barrier, inc=1, device_id=peer(group, r), device_id_type=MESH)
        greeted += PEERS[group]

    loads = []
    sources = [
        (courant, st_cn.at[0]),
        (noise, st_cn.at[1]),
        (gen_cur, st_fields.at[0, pl.ds(0, 3)]),
        (corr_cur, st_fields.at[0, pl.ds(3, 3)]),
        (gen_prev, st_fields.at[1, pl.ds(0, 3)]),
        (corr_prev, st_fields.at[1, pl.ds(3, 3)]),
        (adj_cur, st_fields.at[0, pl.ds(6, 6)]),
        (adj_prev, st_fields.at[1, pl.ds(6, 6)]),
        (owner, v_owner),
        (cell, v_cell),
        (pairs, v_pairs),
        (observed, v_obs),
    ]
    for i, (src, dst) in enumerate(sources):
        copy = pltpu.make_async_copy(src, dst, load_sem.at[i])
        copy.start()
        loads.append(copy)
    lane = lax.broadcasted_iota(jnp.int32, (ROUND, 128), 1)
    sub8 = lax.broadcasted_iota(jnp.int32, (8, 128), 0)
    zeros8 = jnp.zeros((8, 128), F32)

    loads[0].wait()
    loads[1].wait()
    for ch in range(2):
        c2[ch, 0:ROWS] = jnp.concatenate([st_cn[ch, 0], st_cn[ch, 1]], axis=1)
    pl.semaphore_wait(barrier, greeted)

    has_low = lat > 0
    has_high = lat < LATS - 1

    def target(dl, da):
        return ((lon + dl + LONS) % LONS, (lat + da + LATS) % LATS)

    def remote(src, dst, sems, k, dl, da):
        return pltpu.make_async_remote_copy(
            src, dst, sems.at[0, k], sems.at[1, k], device_id=target(dl, da), device_id_type=MESH
        )

    cn_copies = []
    for dl in (-1, 1, -2, 2):
        cn_copies.append(
            (
                remote(
                    c2.at[:, pl.ds(0, ROWS)],
                    cn[-dl].at[:, pl.ds(0, ROWS)],
                    cn_sem,
                    len(cn_copies),
                    dl,
                    0,
                ),
                0,
            )
        )
    for dl in (0, -1, 1, -2, 2):
        for da in (-1, 1):
            cn_copies.append(
                (
                    remote(
                        c2.at[:, pl.ds(0 if da < 0 else 8, 8)],
                        cn_strip.at[0 if da < 0 else 1, 2 - dl],
                        cn_sem,
                        len(cn_copies),
                        dl,
                        da,
                    ),
                    da,
                )
            )

    def sends(da):
        return has_low if da < 0 else has_high

    def receives(da):
        return has_high if da < 0 else has_low

    def go(copies):
        for copy, da in copies:
            if da:
                pl.when(sends(da))(copy.start)
            else:
                copy.start()

    def take(copies):
        for copy, da in copies:
            if da:
                pl.when(receives(da))(copy.wait_recv)
            else:
                copy.wait_recv()

    go(cn_copies)

    for k in range(2, 8):
        loads[k].wait()

    for ch in range(12):
        for t in range(2):
            wide = jnp.concatenate([st_fields[t, ch, 0], st_fields[t, ch, 1]], axis=1)
            fields[1 - t, ch] = wide
    lane16 = lane[0:ROWS]
    row16 = lax.broadcasted_iota(jnp.int32, (ROWS, 128), 0)

    def halo(h):
        copies = []
        for d, dl in enumerate((-1, 1)):
            copies.append(
                (
                    remote(
                        side_out.at[h, d, pl.ds(0, 3 - h)],
                        side_in.at[h, d, pl.ds(0, 3 - h)],
                        halo_sem.at[h],
                        len(copies),
                        dl,
                        0,
                    ),
                    0,
                )
            )
        for d, da in enumerate((-1, 1)):
            copies.append(
                (
                    remote(
                        row_out.at[h, d, pl.ds(0, 3 - h)],
                        row_in.at[h, d, pl.ds(0, 3 - h)],
                        halo_sem.at[h],
                        len(copies),
                        0,
                        da,
                    ),
                    da,
                )
            )
        for d, da in enumerate((-1, 1)):
            for e, dl in enumerate((-1, 1)):
                copies.append(
                    (
                        remote(
                            row_out.at[h, d, 0],
                            corner_in.at[h, d, e],
                            halo_sem.at[h],
                            len(copies),
                            dl,
                            da,
                        ),
                        da,
                    )
                )
        return copies

    def turn(x):
        return pltpu.roll(x, DEEP, 1)

    def send_halo(h):
        n = 2 * h + 1
        for c in range(6):
            one, two = fields[n, c], fields[n, c + 6]
            one_t, two_t = turn(one), turn(two)
            side_out[h, 0, 0, c] = jnp.where(lane16 < DEEP, one, two_t)
            side_out[h, 1, 0, c] = jnp.where(lane16 < DEEP, two_t, one)
            side_out[h, 0, 1, c] = jnp.where(lane16 < DEEP, one_t, two)
            side_out[h, 1, 1, c] = jnp.where(lane16 < DEEP, two, one_t)
            if h == 0:
                one, two_t = fields[n - 1, c], turn(fields[n - 1, c + 6])
                side_out[h, 0, 2, c] = jnp.where(lane16 < DEEP, one, two_t)
                side_out[h, 1, 2, c] = jnp.where(lane16 < DEEP, two_t, one)
        for c in range(12):
            now = fields[n, c]
            row_out[h, 0, 0, c : c + 1] = now[0:1]
            row_out[h, 0, 1, c : c + 1] = now[1:2]
            row_out[h, 1, 0, c : c + 1] = now[ROWS - 1 : ROWS]
            row_out[h, 1, 1, c : c + 1] = now[ROWS - 2 : ROWS - 1]
            if h == 0:
                before = fields[n - 1, c]
                row_out[h, 0, 2, c : c + 1] = before[0:1]
                row_out[h, 1, 2, c : c + 1] = before[ROWS - 1 : ROWS]
        copies = halo(h)
        go(copies)
        return copies

    halos = [send_halo(0)]
    for k in range(8, 12):
        loads[k].wait()

    own = v_owner[...]
    where_in = v_cell[...]
    slon = own * LONG + where_in // (LATS * ROWS * DEEP)
    slat = where_in // DEEP % (LATS * ROWS)
    slane = where_in // (LATS * ROWS * DEEP) * DEEP + where_in % DEEP
    rel_lon = (slon - lon * LONG + 4 + TOTAL_LON) % TOTAL_LON
    rel_lat = slat - lat * ROWS
    near = (rel_lon < 10) & (rel_lat >= -4) & (rel_lat < ROWS + 4)
    row24 = jnp.where(rel_lat < 0, rel_lat + ROUND, rel_lat)
    spot = jnp.where(near, rel_lon // 2 * ROUND + row24, -1)
    spot = jnp.broadcast_to(spot, (ROUND, STATIONS))
    row_id = lax.broadcasted_iota(jnp.int32, (ROUND, STATIONS), 0)
    lanes = lax.broadcasted_iota(jnp.int32, (128, STATIONS), 0)
    hot = jnp.where(lanes == slane, 1.0, 0.0).astype(BF16)
    depth_hot[0:128] = hot
    depth_hot[128:256] = hot

    phase = jnp.broadcast_to(checkpoint[...], (8, 128)).astype(F32)
    weights = [jnp.tile(jnp.cos(OMEGA * (phase + n)), (ROUND // 8, 1)) for n in range(STEPS)]

    ids = lax.broadcasted_iota(jnp.int32, (STATIONS, PAIRS), 0)
    first_hot[...] = jnp.where(ids == v_pairs[0:1], 1.0, 0.0).astype(BF16)
    second_hot[...] = jnp.where(ids == v_pairs[1:2], 1.0, 0.0).astype(BF16)
    rec[...] = jnp.zeros(rec.shape, F32)
    obs[...] = jnp.zeros(obs.shape, F32)
    for n in range(STEPS):
        for i in range(3):
            obs[3 * n + i : 3 * n + i + 1] = v_obs[i, n : n + 1]
    for p in OFFSETS:
        place_hot[p + 2] = jnp.where(spot == row_id + (p + 2) * ROUND, 1.0, 0.0)
    for j in range(8):
        chunks[j, 6:8] = jnp.zeros((2, 128), F32)

    take(cn_copies)
    for p in OFFSETS:
        for ch in range(2):
            above = jnp.where(has_high, cn_strip[0, p + 2, ch], zeros8)
            below = jnp.where(has_low, cn_strip[1, p + 2, ch], zeros8)
            cn[p][ch, ROWS:ROUND] = jnp.where(sub8 < 4, above, below)
    reach = ((-1, 0, 1), (-1, 0, 1), OFFSETS, OFFSETS)

    speed = {p: cn[p][0] for p in OFFSETS}
    hold = {p: 2.0 - 6.0 * speed[p] for p in OFFSETS}
    noisy = [{p: cn[p][1] * weights[n] for p in reach[n]} for n in range(STEPS)]

    def responses(i):
        pad = jnp.zeros((8, 128), F32)

        def own_cells(t, ch):
            return jnp.concatenate([fields[1 - t, ch], pad], axis=0)

        gen = {0: own_cells(0, i)}
        gen_old = {0: own_cells(1, i)}
        corr = {0: own_cells(0, 3 + i)}
        corr_old = {0: own_cells(1, 3 + i)}
        for n in range(STEPS):
            gen_new = advance(gen, gen_old, speed, hold, reach[n], lane)
            corr_new = advance(corr, corr_old, speed, hold, reach[n], lane)
            for p in reach[n]:
                if p in gen:
                    corr_new[p] = corr_new[p] + noisy[n][p] * gen[p]
            gen_old, gen = gen, gen_new
            corr_old, corr = corr, corr_new
            tiles = [field[p] for field in (gen, corr) for p in reach[n]]
            stack = jnp.concatenate(tiles, axis=0)
            picked = dot(jnp.concatenate(split2(stack), axis=1), depth_hot[...])
            for f in range(2):
                summed = jnp.zeros((ROUND, STATIONS), F32)
                for k, p in enumerate(reach[n]):
                    at = (f * len(reach[n]) + k) * ROUND
                    summed = summed + place_hot[p + 2] * picked[at : at + ROUND]
                line = jnp.sum(summed, axis=0, keepdims=True)
                chunks[2 * n + f, i : i + 1] = line[:, 0:128]
                chunks[2 * n + f, 3 + i : 4 + i] = line[:, 128:256]

    for i in range(3):
        responses(i)

    me_xc = block % 4 * 2 + inner % 2

    def post(k, group, src_of, dst_of):
        for r in ORDER[group]:
            pltpu.make_async_remote_copy(
                src_of(r),
                dst_of(r),
                group_sem.at[0, k],
                group_sem.at[1, k],
                device_id=peer(group, r),
                device_id_type=MESH,
            ).start()

    def drain(k, group, side):
        ref = slots.at[k % 3, pl.ds(0, PEERS[group])]
        pltpu.make_async_copy(ref, ref, group_sem.at[side, k]).wait()

    post(0, "xc", lambda r: chunks.at[(me_xc + r) % 8], lambda r: slots.at[0, r - 1])

    def depth_sum(x, lanes):
        deeper = jnp.where(lanes % DEEP == 0, 0.0, pltpu.roll(x, 1, 1))
        higher = jnp.where(lanes % DEEP == DEEP - 1, 0.0, pltpu.roll(x, 127, 1))
        return deeper + higher

    def lat_sum(x, below, above):
        north = jnp.where(row16 == 0, below, pltpu.roll(x, 1, 0))
        south = jnp.where(row16 == ROWS - 1, above, pltpu.roll(x, ROWS - 1, 0))
        return north + south

    def step(n, sides, rows):
        speed = c2[0, 0:ROWS]
        noisy = c2[1, 0:ROWS] * weights[n][0:ROWS]
        for c in range(12):
            x = fields[n + 1, c]
            low, high = sides[0][c % 6], sides[1][c % 6]
            if c < 6:
                along_lon = turn(x + jnp.where(lane16 < DEEP, high, low))
            else:
                along_lon = turn(x) + jnp.where(lane16 < DEEP, low, high)
            near = lat_sum(x, rows[0][c : c + 1], rows[1][c : c + 1])
            around = along_lon + (near + depth_sum(x, lane16)) - 6.0 * x
            new = 2.0 * x - fields[n, c] + speed * around
            if 3 <= c < 6:
                new = new + noisy * fields[n + 1, c - 3]
            fields[n + 2, c] = new

    def layer(h, before):
        n = 2 * h
        arrived = (has_low, has_high)
        row = [
            [jnp.where(arrived[d], row_in[h, 1 - d, j], 0.0) for j in range(3 - h)]
            for d in range(2)
        ]
        if before is None:
            before = (
                [[side_in[h, 1 - e, 2, c] for c in range(6)] for e in range(2)],
                [row[d][2] for d in range(2)],
            )
        corner = [
            [jnp.where(arrived[d], corner_in[h, 1 - d, 1 - e], 0.0) for e in range(2)]
            for d in range(2)
        ]
        sides_now = [[side_in[h, 1 - e, 0, c] for c in range(6)] for e in range(2)]
        sides_new = []
        for e in range(2):
            own_half = lane16 >= DEEP if e == 0 else lane16 < DEEP
            cells = cn[-1 if e == 0 else 1]
            speed = cells[0, 0:ROWS]
            speed = jnp.where(own_half, speed, turn(speed))
            noisy = jnp.where(own_half, cells[1, 0:ROWS] * weights[n][0:ROWS], 0.0)
            ends = [
                jnp.where(own_half, corner[d][e], turn(pltpu.roll(corner[d][e], 10, 0)))
                for d in range(2)
            ]
            new = []
            for c in range(6):
                x = sides_now[e][c]
                along_lon = side_in[h, 1 - e, 1, c] + side_out[h, 1 - e, 1, c]
                near = lat_sum(x, ends[0][c : c + 1], ends[1][c : c + 1])
                around = along_lon + (near + depth_sum(x, lane16)) - 6.0 * x
                v = 2.0 * x - before[0][e][c] + speed * around
                if c >= 3:
                    v = v + noisy * sides_now[e][c - 3]
                new.append(v)
            sides_new.append(new)
        rows_now = [row[d][0] for d in range(2)]
        rows_new = []
        for d in range(2):
            at = ROUND - 1 if d == 0 else ROWS
            x = rows_now[d]
            sides = jnp.where(lane16 < DEEP, corner[d][1], corner[d][0])
            own = row_out[h, d, 0]
            around = turn(x + sides) + (own + row[d][1] + depth_sum(x, lane16)) - 6.0 * x
            v = 2.0 * x - before[1][d] + c2[0, at : at + 1] * around
            moved = jnp.where((row16 >= 3) & (row16 < 6), pltpu.roll(x, 3, 0), 0.0)
            v = v + (c2[1, at : at + 1] * weights[n][0:1]) * moved
            rows_new.append(v)
        return (sides_now, rows_now), (sides_new, rows_new)

    def two_steps(h, before):
        take(halos[h])
        now, new = layer(h, before)
        step(2 * h, *now)
        step(2 * h + 1, *new)
        return new

    shrink = (OFFSETS, (-1, 0, 1), (-1, 0, 1), (0,))

    def gather_sum(k, group, own_part):
        drain(k, group, 1)
        part = own_part
        for r in range(PEERS[group]):
            part = part + slots[k, r]
        total[k] = part
        return part

    gather_sum(0, "xc", chunks[me_xc])
    post(1, "y", lambda r: total.at[0], lambda r: slots.at[1, r - 1])

    kept = two_steps(0, None)
    halos.append(send_halo(1))
    gather_sum(1, "y", total[0])
    post(2, "z", lambda r: total.at[1], lambda r: slots.at[2, r - 1])
    gathered[me_xc] = gather_sum(2, "z", total[1])
    post(3, "xc", lambda r: total.at[2], lambda r: gathered.at[me_xc])
    two_steps(1, kept)
    ref = gathered.at[pl.ds(0, 7)]
    pltpu.make_async_copy(ref, ref, group_sem.at[1, 3]).wait()

    for n in range(STEPS):
        for f in range(2):
            tile = gathered[2 * n + f]
            rec[f, 3 * n : 3 * n + 3, 0:128] = tile[0:3]
            rec[f, 3 * n : 3 * n + 3, 128:256] = tile[3:6]

    def thirds(v, hot, times):
        stack = jnp.concatenate(split3(v), axis=0)
        got = times(stack, hot)
        return got[0:16] + got[16:32] + got[32:48]

    first = first_hot[...]
    second = second_hot[...]
    gen_a = thirds(rec[0], first, dot)
    corr_b = thirds(rec[1], second, dot)
    misfit = gen_a * corr_b - obs[...]
    src = (thirds(misfit * corr_b, first, dot_t), thirds(misfit * gen_a, second, dot_t))

    hot = depth_hot[0:128]
    now = [{} for c in range(6)]
    old = [{} for c in range(6)]
    added = []
    halves = [[h.astype(F32) for h in split2(v)] for v in src]
    for k in range(STEPS):
        later = STEPS - 1 - k
        for c in range(6):
            new = advance(now[c], old[c], speed, hold, shrink[k], lane) if k else {}
            old[c] = now[c]
            line = 3 * later + c % 3
            parts = []
            for h in halves[c // 3]:
                mine = jnp.broadcast_to(h[line : line + 1], (ROUND, STATIONS))
                for p, rows in SPREAD[k]:
                    parts.append(place_hot[p + 2, 0:rows] * mine[0:rows])
            put = dot_t(jnp.concatenate(parts, axis=0).astype(BF16), hot)
            half = put.shape[0] // 2
            both = put[0:half] + put[half:]
            at = 0
            for p, rows in SPREAD[k]:
                piece = both[at : at + rows]
                if rows < ROUND:
                    piece = jnp.concatenate([piece, jnp.zeros((ROUND - rows, 128), F32)], axis=0)
                new[p] = new[p] + piece if k else piece
                at += rows
            now[c] = new
        added.append([now[c][0][0:ROWS] for c in range(6)])

    kernel = jnp.zeros((ROWS, 128), F32)
    for k in range(STEPS):
        for c in range(3):
            kernel = kernel + (fields[k + 2, 9 + c] + added[k][3 + c]) * fields[STEPS + 1 - k, c]
    for c in range(3):
        last = fields[STEPS + 1, 3 + c]
        out_corr[c, 0] = last[:, 0:DEEP]
        out_corr[c, 1] = last[:, DEEP:128]
    for c in range(6):
        last = fields[STEPS + 1, 6 + c] + added[STEPS - 1][c]
        out_adj[c, 0] = last[:, 0:DEEP]
        out_adj[c, 1] = last[:, DEEP:128]
    out_kernel[0] = kernel[:, 0:DEEP]
    out_kernel[1] = kernel[:, DEEP:128]

    for copies in [cn_copies] + halos:
        for copy, da in copies:
            if da:
                pl.when(sends(da))(copy.wait_send)
            else:
                copy.wait_send()
    for k, group in enumerate(("xc", "y", "z", "xc")):
        drain(k, group, 0)


def hand_over(corr, adj, kernel, out_corr, out_adj, out_kernel):
    out_corr[...] = corr[...]
    out_adj[...] = adj[...]
    out_kernel[...] = kernel[...]


def shards(
    gen_prev,
    gen_cur,
    corr_prev,
    corr_cur,
    adj_prev,
    adj_cur,
    courant,
    noise,
    station_owner,
    station_cell,
    pairs,
    observed,
    checkpoint,
):
    anywhere = pl.BlockSpec(memory_space=pltpu.HBM)
    vmem = pl.BlockSpec(memory_space=pltpu.VMEM)
    cn = pltpu.VMEM((2, ROUND, 128), F32)
    results = pl.pallas_call(
        body,
        name="window",
        out_shape=(
            jax.ShapeDtypeStruct((3, LONG, ROWS, DEEP), F32),
            jax.ShapeDtypeStruct((6, LONG, ROWS, DEEP), F32),
            jax.ShapeDtypeStruct((LONG, ROWS, DEEP), F32),
        ),
        in_specs=[anywhere] * 12 + [vmem],
        out_specs=(vmem, vmem, vmem),
        scratch_shapes=[
            pltpu.VMEM((2, 12, LONG, ROWS, DEEP), F32),
            pltpu.VMEM((2, LONG, ROWS, DEEP), F32),
            pltpu.VMEM((1, STATIONS), jnp.int32),
            pltpu.VMEM((1, STATIONS), jnp.int32),
            pltpu.VMEM((2, PAIRS), jnp.int32),
            pltpu.VMEM((3, STEPS, PAIRS), F32),
            pltpu.VMEM((STEPS + 2, 12, ROWS, 128), F32),
            cn,
            cn,
            cn,
            cn,
            cn,
            pltpu.VMEM((2, 5, 2, 8, 128), F32),
            pltpu.VMEM((2, 2, 3, 6, ROWS, 128), F32),
            pltpu.VMEM((2, 2, 3, 6, ROWS, 128), F32),
            pltpu.VMEM((2, 2, 3, 16, 128), F32),
            pltpu.VMEM((2, 2, 3, 16, 128), F32),
            pltpu.VMEM((2, 2, 2, 16, 128), F32),
            pltpu.VMEM((5, ROUND, STATIONS), F32),
            pltpu.VMEM((256, STATIONS), BF16),
            pltpu.VMEM((STATIONS, PAIRS), BF16),
            pltpu.VMEM((STATIONS, PAIRS), BF16),
            pltpu.VMEM((16, PAIRS), F32),
            pltpu.VMEM((8, 8, 128), F32),
            pltpu.VMEM((3, 8, 128), F32),
            pltpu.VMEM((3, 11, 8, 128), F32),
            pltpu.VMEM((8, 8, 128), F32),
            pltpu.VMEM((2, 16, STATIONS), F32),
            pltpu.SemaphoreType.DMA((12,)),
            pltpu.SemaphoreType.DMA((2, 14)),
            pltpu.SemaphoreType.DMA((2, 2, 8)),
            pltpu.SemaphoreType.DMA((2, 4)),
        ],
        compiler_params=pltpu.CompilerParams(
            collective_id=0, has_side_effects=True, vmem_limit_bytes=56 * 1024 * 1024
        ),
    )(
        gen_prev,
        gen_cur,
        corr_prev,
        corr_cur,
        adj_prev,
        adj_cur,
        courant,
        noise,
        station_owner.reshape(1, STATIONS),
        station_cell.reshape(1, STATIONS),
        pairs,
        jnp.transpose(observed, (1, 0, 2)),
        checkpoint.reshape(1, 1),
    )
    return pl.pallas_call(
        hand_over,
        name="results",
        out_shape=tuple(jax.ShapeDtypeStruct(r.shape, r.dtype) for r in results),
        in_specs=[vmem] * 3,
        out_specs=(vmem,) * 3,
        compiler_params=pltpu.CompilerParams(vmem_limit_bytes=56 * 1024 * 1024),
    )(*results)


def solution(mesh):
    field = P(None, "lon", "lat", None)
    cells = P("lon", "lat", None)
    return jax.shard_map(
        shards,
        mesh=mesh,
        in_specs=(field,) * 6 + (cells,) * 2 + (P(),) * 5,
        out_specs=(field, field, cells),
        check_vma=False,
    )
```

```python
import jax
import jax.numpy as jnp
from jax import lax
from jax.experimental import pallas as pl
from jax.experimental.pallas import tpu as pltpu
from jax.sharding import PartitionSpec as P

OMEGA = 0.7
MESH = pl.DeviceIdType.MESH
F32 = jnp.float32
BF16 = jnp.bfloat16
LONS = 192
LATS = 4
RING_Z = 12
LONG = 2
ROWS = 16
DEEP = 64
TOTAL_LON = LONS * LONG
ROUND = 24
STEPS = 4
STATIONS = 256
PAIRS = 1024
STRIPS = (-1, 0, 1)
OFFSETS = (-2, -1, 0, 1, 2)
SPREAD = (
    ((0, 24), (-1, 24), (1, 24), (-2, 16), (2, 16)),
    ((0, 24), (-1, 24), (1, 24)),
    ((0, 24), (-1, 16), (1, 16)),
    ((0, 16),),
)
GROUPS = ("z", "y", "xc")
PEERS = {"xc": 7, "y": 7, "z": 11}
ORDER = {
    "xc": (4, 3, 5, 2, 6, 1, 7),
    "y": (4, 3, 5, 2, 6, 1, 7),
    "z": (6, 5, 7, 4, 8, 3, 9, 2, 10, 1, 11),
}


def place():
    lon = lax.axis_index("lon")
    lat = lax.axis_index("lat")
    return lon, lat, lon // 24, lon % 24


def peer(group, r):
    lon, lat, block, inner = place()
    if group == "xc":
        t = (block % 4 * 2 + inner % 2 + r) % 8
        return ((block // 4 * 4 + t // 2) * 24 + inner // 2 * 2 + t % 2, lat)
    if group == "y":
        t = (block // 4 * 4 + lat + r) % 8
        return ((t // 4 * 4 + block % 4) * 24 + inner, t % 4)
    return (block * 24 + (inner + 2 * r) % 24, lat)


def split2(v):
    high = v.astype(BF16)
    return high, (v - high.astype(F32)).astype(BF16)


def dot(a, b):
    return lax.dot_general(a, b, (((1,), (0,)), ((), ())), preferred_element_type=F32)


def dot_t(a, b):
    return lax.dot_general(a, b, (((1,), (1,)), ((), ())), preferred_element_type=F32)


def around(cur, p, lane):
    x = cur.get(p)
    low = cur.get(p - 1)
    high = cur.get(p + 1)
    zero = jnp.zeros((ROUND, 128), F32)
    sides = jnp.where(
        lane >= DEEP, zero if low is None else low, zero if high is None else high
    )
    if x is None:
        return pltpu.roll(sides, DEEP, 1)
    along_lon = pltpu.roll(x + sides, DEEP, 1)
    deeper = jnp.where(lane % DEEP == 0, 0.0, pltpu.roll(x, 1, 1))
    higher = jnp.where(lane % DEEP == DEEP - 1, 0.0, pltpu.roll(x, 127, 1))
    north = pltpu.roll(x, 1, 0)
    south = pltpu.roll(x, ROUND - 1, 0)
    return along_lon + (north + south + deeper + higher)


def advance(cur, old, speed, hold, pairs, lane):
    new = {}
    for p in pairs:
        v = speed[p] * around(cur, p, lane)
        if p in cur:
            v = v + hold[p] * cur[p]
        if p in old:
            v = v - old[p]
        new[p] = v
    return new


def body(
    gen_prev,
    gen_cur,
    corr_prev,
    corr_cur,
    adj_prev,
    adj_cur,
    courant,
    noise,
    owner,
    cell,
    pairs,
    observed,
    checkpoint,
    out_corr,
    out_adj,
    out_kernel,
    st_fields,
    st_cn,
    v_owner,
    v_cell,
    v_pairs,
    v_obs,
    fields,
    c0,
    c1,
    c2,
    c3,
    c4,
    cn_strip,
    side_out,
    side_in,
    row_out,
    row_in,
    corner_in,
    place_hot,
    depth_hot,
    first_hot,
    second_hot,
    obs,
    chunks,
    total,
    slots,
    gathered,
    rec,
    load_sem,
    cn_sem,
    halo_sem,
    group_sem,
):
    lon, lat, block, inner = place()
    cn = {-2: c0, -1: c1, 0: c2, 1: c3, 2: c4}
    barrier = pltpu.get_barrier_semaphore()
    greeted = 0
    for dl in OFFSETS:
        for da in STRIPS:
            if dl or da:
                pl.semaphore_signal(
                    barrier,
                    inc=1,
                    device_id=((lon + dl + LONS) % LONS, (lat + da + LATS) % LATS),
                    device_id_type=MESH,
                )
                greeted += 1
    for group in GROUPS:
        for r in ORDER[group]:
            pl.semaphore_signal(barrier, inc=1, device_id=peer(group, r), device_id_type=MESH)
        greeted += PEERS[group]

    loads = []
    sources = [
        (courant, st_cn.at[0]),
        (noise, st_cn.at[1]),
        (gen_cur, st_fields.at[0, pl.ds(0, 3)]),
        (corr_cur, st_fields.at[0, pl.ds(3, 3)]),
        (gen_prev, st_fields.at[1, pl.ds(0, 3)]),
        (corr_prev, st_fields.at[1, pl.ds(3, 3)]),
        (adj_cur, st_fields.at[0, pl.ds(6, 6)]),
        (adj_prev, st_fields.at[1, pl.ds(6, 6)]),
        (owner, v_owner),
        (cell, v_cell),
        (pairs, v_pairs),
        (observed, v_obs),
    ]
    for i, (src, dst) in enumerate(sources):
        copy = pltpu.make_async_copy(src, dst, load_sem.at[i])
        copy.start()
        loads.append(copy)
    lane = lax.broadcasted_iota(jnp.int32, (ROUND, 128), 1)
    sub8 = lax.broadcasted_iota(jnp.int32, (8, 128), 0)
    zeros8 = jnp.zeros((8, 128), F32)

    loads[0].wait()
    loads[1].wait()
    for ch in range(2):
        c2[ch, 0:ROWS] = jnp.concatenate([st_cn[ch, 0], st_cn[ch, 1]], axis=1)
    pl.semaphore_wait(barrier, greeted)

    has_low = lat > 0
    has_high = lat < LATS - 1

    def target(dl, da):
        return ((lon + dl + LONS) % LONS, (lat + da + LATS) % LATS)

    def remote(src, dst, sems, k, dl, da):
        return pltpu.make_async_remote_copy(
            src, dst, sems.at[0, k], sems.at[1, k], device_id=target(dl, da), device_id_type=MESH
        )

    cn_copies = []
    for dl in (-1, 1, -2, 2):
        cn_copies.append(
            (
                remote(
                    c2.at[:, pl.ds(0, ROWS)],
                    cn[-dl].at[:, pl.ds(0, ROWS)],
                    cn_sem,
                    len(cn_copies),
                    dl,
                    0,
                ),
                0,
            )
        )
    for dl in (0, -1, 1, -2, 2):
        for da in (-1, 1):
            cn_copies.append(
                (
                    remote(
                        c2.at[:, pl.ds(0 if da < 0 else 8, 8)],
                        cn_strip.at[0 if da < 0 else 1, 2 - dl],
                        cn_sem,
                        len(cn_copies),
                        dl,
                        da,
                    ),
                    da,
                )
            )

    def sends(da):
        return has_low if da < 0 else has_high

    def receives(da):
        return has_high if da < 0 else has_low

    def go(copies):
        for copy, da in copies:
            if da:
                pl.when(sends(da))(copy.start)
            else:
                copy.start()

    def take(copies):
        for copy, da in copies:
            if da:
                pl.when(receives(da))(copy.wait_recv)
            else:
                copy.wait_recv()

    go(cn_copies)

    for k in range(2, 8):
        loads[k].wait()

    for ch in range(12):
        for t in range(2):
            wide = jnp.concatenate([st_fields[t, ch, 0], st_fields[t, ch, 1]], axis=1)
            fields[1 - t, ch] = wide
    lane16 = lane[0:ROWS]
    row16 = lax.broadcasted_iota(jnp.int32, (ROWS, 128), 0)

    def halo(h):
        copies = []
        for d, dl in enumerate((-1, 1)):
            copies.append(
                (
                    remote(
                        side_out.at[h, d, pl.ds(0, 3 - h)],
                        side_in.at[h, d, pl.ds(0, 3 - h)],
                        halo_sem.at[h],
                        len(copies),
                        dl,
                        0,
                    ),
                    0,
                )
            )
        for d, da in enumerate((-1, 1)):
            copies.append(
                (
                    remote(
                        row_out.at[h, d, pl.ds(0, 3 - h)],
                        row_in.at[h, d, pl.ds(0, 3 - h)],
                        halo_sem.at[h],
                        len(copies),
                        0,
                        da,
                    ),
                    da,
                )
            )
        for d, da in enumerate((-1, 1)):
            for e, dl in enumerate((-1, 1)):
                copies.append(
                    (
                        remote(
                            row_out.at[h, d, 0],
                            corner_in.at[h, d, e],
                            halo_sem.at[h],
                            len(copies),
                            dl,
                            da,
                        ),
                        da,
                    )
                )
        return copies

    def turn(x):
        return pltpu.roll(x, DEEP, 1)

    def send_halo(h):
        n = 2 * h + 1
        for c in range(6):
            one, two = fields[n, c], fields[n, c + 6]
            one_t, two_t = turn(one), turn(two)
            side_out[h, 0, 0, c] = jnp.where(lane16 < DEEP, one, two_t)
            side_out[h, 1, 0, c] = jnp.where(lane16 < DEEP, two_t, one)
            side_out[h, 0, 1, c] = jnp.where(lane16 < DEEP, one_t, two)
            side_out[h, 1, 1, c] = jnp.where(lane16 < DEEP, two, one_t)
            if h == 0:
                one, two_t = fields[n - 1, c], turn(fields[n - 1, c + 6])
                side_out[h, 0, 2, c] = jnp.where(lane16 < DEEP, one, two_t)
                side_out[h, 1, 2, c] = jnp.where(lane16 < DEEP, two_t, one)
        for c in range(12):
            now = fields[n, c]
            row_out[h, 0, 0, c : c + 1] = now[0:1]
            row_out[h, 0, 1, c : c + 1] = now[1:2]
            row_out[h, 1, 0, c : c + 1] = now[ROWS - 1 : ROWS]
            row_out[h, 1, 1, c : c + 1] = now[ROWS - 2 : ROWS - 1]
            if h == 0:
                before = fields[n - 1, c]
                row_out[h, 0, 2, c : c + 1] = before[0:1]
                row_out[h, 1, 2, c : c + 1] = before[ROWS - 1 : ROWS]
        copies = halo(h)
        go(copies)
        return copies

    halos = [send_halo(0)]
    for k in range(8, 12):
        loads[k].wait()

    own = v_owner[...]
    where_in = v_cell[...]
    slon = own * LONG + where_in // (LATS * ROWS * DEEP)
    slat = where_in // DEEP % (LATS * ROWS)
    slane = where_in // (LATS * ROWS * DEEP) * DEEP + where_in % DEEP
    rel_lon = (slon - lon * LONG + 4 + TOTAL_LON) % TOTAL_LON
    rel_lat = slat - lat * ROWS
    near = (rel_lon < 10) & (rel_lat >= -4) & (rel_lat < ROWS + 4)
    row24 = jnp.where(rel_lat < 0, rel_lat + ROUND, rel_lat)
    spot = jnp.where(near, rel_lon // 2 * ROUND + row24, -1)
    spot = jnp.broadcast_to(spot, (ROUND, STATIONS))
    row_id = lax.broadcasted_iota(jnp.int32, (ROUND, STATIONS), 0)
    lanes = lax.broadcasted_iota(jnp.int32, (128, STATIONS), 0)
    hot = jnp.where(lanes == slane, 1.0, 0.0).astype(BF16)
    depth_hot[0:128] = hot
    depth_hot[128:256] = hot

    phase = jnp.broadcast_to(checkpoint[...], (8, 128)).astype(F32)
    weights = [jnp.tile(jnp.cos(OMEGA * (phase + n)), (ROUND // 8, 1)) for n in range(STEPS)]

    ids = lax.broadcasted_iota(jnp.int32, (STATIONS, PAIRS), 0)
    first_hot[...] = jnp.where(ids == v_pairs[0:1], 1.0, 0.0).astype(BF16)
    second_hot[...] = jnp.where(ids == v_pairs[1:2], 1.0, 0.0).astype(BF16)
    rec[...] = jnp.zeros(rec.shape, F32)
    obs[...] = jnp.zeros(obs.shape, F32)
    for n in range(STEPS):
        for i in range(3):
            obs[3 * n + i : 3 * n + i + 1] = v_obs[i, n : n + 1]
    for p in OFFSETS:
        place_hot[p + 2] = jnp.where(spot == row_id + (p + 2) * ROUND, 1.0, 0.0)

    take(cn_copies)
    for p in OFFSETS:
        for ch in range(2):
            above = jnp.where(has_high, cn_strip[0, p + 2, ch], zeros8)
            below = jnp.where(has_low, cn_strip[1, p + 2, ch], zeros8)
            cn[p][ch, ROWS:ROUND] = jnp.where(sub8 < 4, above, below)
    reach = ((-1, 0, 1), (-1, 0, 1), OFFSETS, OFFSETS)

    speed = {p: cn[p][0] for p in OFFSETS}
    hold = {p: 2.0 - 6.0 * speed[p] for p in OFFSETS}
    noisy = [{p: cn[p][1] * weights[n] for p in reach[n]} for n in range(STEPS)]

    def responses(i):
        pad = jnp.zeros((8, 128), F32)

        def own_cells(t, ch):
            return jnp.concatenate([fields[1 - t, ch], pad], axis=0)

        gen = {0: own_cells(0, i)}
        gen_old = {0: own_cells(1, i)}
        corr = {0: own_cells(0, 3 + i)}
        corr_old = {0: own_cells(1, 3 + i)}
        for n in range(STEPS):
            gen_new = advance(gen, gen_old, speed, hold, reach[n], lane)
            corr_new = advance(corr, corr_old, speed, hold, reach[n], lane)
            for p in reach[n]:
                if p in gen:
                    corr_new[p] = corr_new[p] + noisy[n][p] * gen[p]
            gen_old, gen = gen, gen_new
            corr_old, corr = corr, corr_new
            tiles = [field[p] for field in (gen, corr) for p in reach[n]]
            stack = jnp.concatenate(tiles, axis=0)
            picked = dot(jnp.concatenate(split2(stack), axis=1), depth_hot[...])
            for f in range(2):
                summed = jnp.zeros((ROUND, STATIONS), F32)
                for k, p in enumerate(reach[n]):
                    at = (f * len(reach[n]) + k) * ROUND
                    summed = summed + place_hot[p + 2] * picked[at : at + ROUND]
                line = jnp.sum(summed, axis=0, keepdims=True)
                chunks[2 * n + f, i : i + 1] = line[:, 0:128]
                chunks[2 * n + f, 3 + i : 4 + i] = line[:, 128:256]

    for i in range(3):
        responses(i)

    me_xc = block % 4 * 2 + inner % 2
    held = pl.ds(0, 6)

    def post(k, group, src_of, dst_of):
        for r in ORDER[group]:
            pltpu.make_async_remote_copy(
                src_of(r),
                dst_of(r),
                group_sem.at[0, k],
                group_sem.at[1, k],
                device_id=peer(group, r),
                device_id_type=MESH,
            ).start()

    def drain(k, group, side):
        ref = slots.at[k % 3, pl.ds(0, PEERS[group]), held]
        pltpu.make_async_copy(ref, ref, group_sem.at[side, k]).wait()

    post(0, "xc", lambda r: chunks.at[(me_xc + r) % 8, held], lambda r: slots.at[0, r - 1, held])

    def depth_sum(x, lanes):
        deeper = jnp.where(lanes % DEEP == 0, 0.0, pltpu.roll(x, 1, 1))
        higher = jnp.where(lanes % DEEP == DEEP - 1, 0.0, pltpu.roll(x, 127, 1))
        return deeper + higher

    def lat_sum(x, below, above):
        north = jnp.where(row16 == 0, below, pltpu.roll(x, 1, 0))
        south = jnp.where(row16 == ROWS - 1, above, pltpu.roll(x, ROWS - 1, 0))
        return north + south

    def step(n, sides, rows):
        speed = c2[0, 0:ROWS]
        noisy = c2[1, 0:ROWS] * weights[n][0:ROWS]
        for c in range(12):
            x = fields[n + 1, c]
            low, high = sides[0][c % 6], sides[1][c % 6]
            if c < 6:
                along_lon = turn(x + jnp.where(lane16 < DEEP, high, low))
            else:
                along_lon = turn(x) + jnp.where(lane16 < DEEP, low, high)
            near = lat_sum(x, rows[0][c : c + 1], rows[1][c : c + 1])
            around = along_lon + (near + depth_sum(x, lane16)) - 6.0 * x
            new = 2.0 * x - fields[n, c] + speed * around
            if 3 <= c < 6:
                new = new + noisy * fields[n + 1, c - 3]
            fields[n + 2, c] = new

    def layer(h, before):
        n = 2 * h
        arrived = (has_low, has_high)
        row = [
            [jnp.where(arrived[d], row_in[h, 1 - d, j], 0.0) for j in range(3 - h)]
            for d in range(2)
        ]
        if before is None:
            before = (
                [[side_in[h, 1 - e, 2, c] for c in range(6)] for e in range(2)],
                [row[d][2] for d in range(2)],
            )
        corner = [
            [jnp.where(arrived[d], corner_in[h, 1 - d, 1 - e], 0.0) for e in range(2)]
            for d in range(2)
        ]
        sides_now = [[side_in[h, 1 - e, 0, c] for c in range(6)] for e in range(2)]
        sides_new = []
        for e in range(2):
            own_half = lane16 >= DEEP if e == 0 else lane16 < DEEP
            cells = cn[-1 if e == 0 else 1]
            speed = cells[0, 0:ROWS]
            speed = jnp.where(own_half, speed, turn(speed))
            noisy = jnp.where(own_half, cells[1, 0:ROWS] * weights[n][0:ROWS], 0.0)
            ends = [
                jnp.where(own_half, corner[d][e], turn(pltpu.roll(corner[d][e], 10, 0)))
                for d in range(2)
            ]
            new = []
            for c in range(6):
                x = sides_now[e][c]
                along_lon = side_in[h, 1 - e, 1, c] + side_out[h, 1 - e, 1, c]
                near = lat_sum(x, ends[0][c : c + 1], ends[1][c : c + 1])
                around = along_lon + (near + depth_sum(x, lane16)) - 6.0 * x
                v = 2.0 * x - before[0][e][c] + speed * around
                if c >= 3:
                    v = v + noisy * sides_now[e][c - 3]
                new.append(v)
            sides_new.append(new)
        rows_now = [row[d][0] for d in range(2)]
        rows_new = []
        for d in range(2):
            at = ROUND - 1 if d == 0 else ROWS
            x = rows_now[d]
            sides = jnp.where(lane16 < DEEP, corner[d][1], corner[d][0])
            own = row_out[h, d, 0]
            around = turn(x + sides) + (own + row[d][1] + depth_sum(x, lane16)) - 6.0 * x
            v = 2.0 * x - before[1][d] + c2[0, at : at + 1] * around
            moved = jnp.where((row16 >= 3) & (row16 < 6), pltpu.roll(x, 3, 0), 0.0)
            v = v + (c2[1, at : at + 1] * weights[n][0:1]) * moved
            rows_new.append(v)
        return (sides_now, rows_now), (sides_new, rows_new)

    def two_steps(h, before):
        take(halos[h])
        now, new = layer(h, before)
        step(2 * h, *now)
        step(2 * h + 1, *new)
        return new

    shrink = (OFFSETS, (-1, 0, 1), (-1, 0, 1), (0,))

    def gather_sum(k, group, own_part):
        drain(k, group, 1)
        part = own_part
        for r in range(PEERS[group]):
            part = part + slots[k, r, 0:6]
        total[k, 0:6] = part
        return part

    gather_sum(0, "xc", chunks[me_xc, 0:6])
    post(1, "y", lambda r: total.at[0, held], lambda r: slots.at[1, r - 1, held])

    kept = two_steps(0, None)
    halos.append(send_halo(1))
    gather_sum(1, "y", total[0, 0:6])
    post(2, "z", lambda r: total.at[1, held], lambda r: slots.at[2, r - 1, held])
    gathered[me_xc, 0:6] = gather_sum(2, "z", total[1, 0:6])
    post(3, "xc", lambda r: total.at[2, held], lambda r: gathered.at[me_xc, held])
    two_steps(1, kept)
    ref = gathered.at[pl.ds(0, 7), held]
    pltpu.make_async_copy(ref, ref, group_sem.at[1, 3]).wait()

    for n in range(STEPS):
        for f in range(2):
            tile = gathered[2 * n + f]
            rec[f, 3 * n : 3 * n + 3, 0:128] = tile[0:3]
            rec[f, 3 * n : 3 * n + 3, 128:256] = tile[3:6]

    def parted(v, hot, times):
        stack = jnp.concatenate(split2(v), axis=0)
        got = times(stack, hot)
        return got[0:16] + got[16:32]

    first = first_hot[...]
    second = second_hot[...]
    gen_a = parted(rec[0], first, dot)
    corr_b = parted(rec[1], second, dot)
    misfit = gen_a * corr_b - obs[...]
    src = (parted(misfit * corr_b, first, dot_t), parted(misfit * gen_a, second, dot_t))

    hot = depth_hot[0:128]
    now = [{} for c in range(6)]
    old = [{} for c in range(6)]
    added = []
    halves = [[h.astype(F32) for h in split2(v)] for v in src]
    for k in range(STEPS):
        later = STEPS - 1 - k
        for c in range(6):
            new = advance(now[c], old[c], speed, hold, shrink[k], lane) if k else {}
            old[c] = now[c]
            line = 3 * later + c % 3
            parts = []
            for h in halves[c // 3]:
                mine = jnp.broadcast_to(h[line : line + 1], (ROUND, STATIONS))
                for p, rows in SPREAD[k]:
                    parts.append(place_hot[p + 2, 0:rows] * mine[0:rows])
            put = dot_t(jnp.concatenate(parts, axis=0).astype(BF16), hot)
            half = put.shape[0] // 2
            both = put[0:half] + put[half:]
            at = 0
            for p, rows in SPREAD[k]:
                piece = both[at : at + rows]
                if rows < ROUND:
                    piece = jnp.concatenate([piece, jnp.zeros((ROUND - rows, 128), F32)], axis=0)
                new[p] = new[p] + piece if k else piece
                at += rows
            now[c] = new
        added.append([now[c][0][0:ROWS] for c in range(6)])

    kernel = jnp.zeros((ROWS, 128), F32)
    for k in range(STEPS):
        for c in range(3):
            kernel = kernel + (fields[k + 2, 9 + c] + added[k][3 + c]) * fields[STEPS + 1 - k, c]
    for c in range(3):
        last = fields[STEPS + 1, 3 + c]
        out_corr[c, 0] = last[:, 0:DEEP]
        out_corr[c, 1] = last[:, DEEP:128]
    for c in range(6):
        last = fields[STEPS + 1, 6 + c] + added[STEPS - 1][c]
        out_adj[c, 0] = last[:, 0:DEEP]
        out_adj[c, 1] = last[:, DEEP:128]
    out_kernel[0] = kernel[:, 0:DEEP]
    out_kernel[1] = kernel[:, DEEP:128]

    for copies in [cn_copies] + halos:
        for copy, da in copies:
            if da:
                pl.when(sends(da))(copy.wait_send)
            else:
                copy.wait_send()
    for k, group in enumerate(("xc", "y", "z", "xc")):
        drain(k, group, 0)


def hand_over(corr, adj, kernel, out_corr, out_adj, out_kernel):
    out_corr[...] = corr[...]
    out_adj[...] = adj[...]
    out_kernel[...] = kernel[...]


def shards(
    gen_prev,
    gen_cur,
    corr_prev,
    corr_cur,
    adj_prev,
    adj_cur,
    courant,
    noise,
    station_owner,
    station_cell,
    pairs,
    observed,
    checkpoint,
):
    anywhere = pl.BlockSpec(memory_space=pltpu.HBM)
    vmem = pl.BlockSpec(memory_space=pltpu.VMEM)
    cn = pltpu.VMEM((2, ROUND, 128), F32)
    results = pl.pallas_call(
        body,
        name="window",
        out_shape=(
            jax.ShapeDtypeStruct((3, LONG, ROWS, DEEP), F32),
            jax.ShapeDtypeStruct((6, LONG, ROWS, DEEP), F32),
            jax.ShapeDtypeStruct((LONG, ROWS, DEEP), F32),
        ),
        in_specs=[anywhere] * 12 + [vmem],
        out_specs=(vmem, vmem, vmem),
        scratch_shapes=[
            pltpu.VMEM((2, 12, LONG, ROWS, DEEP), F32),
            pltpu.VMEM((2, LONG, ROWS, DEEP), F32),
            pltpu.VMEM((1, STATIONS), jnp.int32),
            pltpu.VMEM((1, STATIONS), jnp.int32),
            pltpu.VMEM((2, PAIRS), jnp.int32),
            pltpu.VMEM((3, STEPS, PAIRS), F32),
            pltpu.VMEM((STEPS + 2, 12, ROWS, 128), F32),
            cn,
            cn,
            cn,
            cn,
            cn,
            pltpu.VMEM((2, 5, 2, 8, 128), F32),
            pltpu.VMEM((2, 2, 3, 6, ROWS, 128), F32),
            pltpu.VMEM((2, 2, 3, 6, ROWS, 128), F32),
            pltpu.VMEM((2, 2, 3, 16, 128), F32),
            pltpu.VMEM((2, 2, 3, 16, 128), F32),
            pltpu.VMEM((2, 2, 2, 16, 128), F32),
            pltpu.VMEM((5, ROUND, STATIONS), F32),
            pltpu.VMEM((256, STATIONS), BF16),
            pltpu.VMEM((STATIONS, PAIRS), BF16),
            pltpu.VMEM((STATIONS, PAIRS), BF16),
            pltpu.VMEM((16, PAIRS), F32),
            pltpu.VMEM((8, 8, 128), F32),
            pltpu.VMEM((3, 8, 128), F32),
            pltpu.VMEM((3, 11, 8, 128), F32),
            pltpu.VMEM((8, 8, 128), F32),
            pltpu.VMEM((2, 16, STATIONS), F32),
            pltpu.SemaphoreType.DMA((12,)),
            pltpu.SemaphoreType.DMA((2, 14)),
            pltpu.SemaphoreType.DMA((2, 2, 8)),
            pltpu.SemaphoreType.DMA((2, 4)),
        ],
        compiler_params=pltpu.CompilerParams(
            collective_id=0, has_side_effects=True, vmem_limit_bytes=56 * 1024 * 1024
        ),
    )(
        gen_prev,
        gen_cur,
        corr_prev,
        corr_cur,
        adj_prev,
        adj_cur,
        courant,
        noise,
        station_owner.reshape(1, STATIONS),
        station_cell.reshape(1, STATIONS),
        pairs,
        jnp.transpose(observed, (1, 0, 2)),
        checkpoint.reshape(1, 1),
    )
    return pl.pallas_call(
        hand_over,
        name="results",
        out_shape=tuple(jax.ShapeDtypeStruct(r.shape, r.dtype) for r in results),
        in_specs=[vmem] * 3,
        out_specs=(vmem,) * 3,
        compiler_params=pltpu.CompilerParams(vmem_limit_bytes=56 * 1024 * 1024),
    )(*results)


def solution(mesh):
    field = P(None, "lon", "lat", None)
    cells = P("lon", "lat", None)
    return jax.shard_map(
        shards,
        mesh=mesh,
        in_specs=(field,) * 6 + (cells,) * 2 + (P(),) * 5,
        out_specs=(field, field, cells),
        check_vma=False,
    )
```
